256 devices in a mesh: ctx: 8 (over y, x_hi), head: 32 (over z, x_lo, core).
Axes of the slice: x: 4 (x_hi: 2, x_lo: 2; x = x_hi * 2 + x_lo), y: 4, z: 8, core: 2. Of those that a mesh axis runs over, the one named last changes fastest.
Arguments:
- queries: bfloat16 [2048, 128, 128], P('ctx', 'head'), may hold values from -24 to 24
- cache_keys: bfloat16 [8, 6144, 128], P(None, 'ctx'), may hold values from -12 to 12
- cache_values: bfloat16 [8, 6144, 128], P(None, 'ctx'), may hold values from -6 to 6
- scale_index: int32 [8, 48], P(None, 'ctx'), may hold values from 0 to 63
- scale_table: float32 [2, 64], replicated, may hold values from 0.6 to 1.6
- hist_lengths: int32 [8], P('ctx'), may hold values from 192 to 768, as said below
- span_offsets: int32 [16], replicated, may hold values from 0 to 6144
- new_keys: bfloat16 [2048, 8, 128], P('ctx'), may hold values from -12 to 12
- new_values: bfloat16 [2048, 8, 128], P('ctx'), may hold values from -6 to 6
- head_groups: int32 [128], P('head'), may hold values from 0 to 7, as said below
- out_weight: bfloat16 [16384, 8192], P('head'), may hold values from -0.75 to 0.75
Outputs:
- projected: bfloat16 [2048, 8192], P('ctx', 'head')
The draws below stay inside these ranges and needn't reach their ends.
Inputs may be any that keep to these rules, and one draw needn't show every extreme that they name: `head_groups`: each key-value head serves exactly 16 query heads. `hist_lengths`: at least one block is full.
All inputs are finite; a program needn't handle non-finite values.
Results may differ from the reference program's by a relative error of at most 0.0058.
Values may be sent and summed in bfloat16 or wider, within the bound.
No kernel may reach another device: no remote copies, remote signals or barrier semaphores. Data moves between devices by JAX's collectives and lax.ppermute only.
A program may use at most 64 MiB of HBM per device.

```python
import math
import jax
import jax.numpy as jnp
from jax import lax

H = 128
KVH = 8
DH = 128
D_OUT = 8192
HISTORY_SLOTS = 768
SPAN = 128
SBLK = 128
NSCALE = 64
QROWS = 2048
SPANS = 16
SLOTS = 6144
NBLK = 48
N_CTX = 8


def draw_queries(key, part):
    key = jax.random.fold_in(key, 11)
    values = jax.random.normal(key, (QROWS, H, DH), jnp.float32)
    return jnp.clip(values, -24.0, 24.0).astype(jnp.bfloat16)


def draw_cache_keys(key, part):
    key = jax.random.fold_in(key, 12)
    values = jax.random.normal(key, (KVH, SLOTS, DH), jnp.float32)
    return jnp.clip(values, -12.0, 12.0).astype(jnp.bfloat16)


def draw_new_keys(key, part):
    key = jax.random.fold_in(key, 13)
    values = jax.random.normal(key, (QROWS, KVH, DH), jnp.float32)
    return jnp.clip(values, -12.0, 12.0).astype(jnp.bfloat16)


def draw_hist_lengths(key, part):
    key = jax.random.fold_in(key, 14)
    counts = jax.random.randint(key, (N_CTX,), HISTORY_SLOTS // 4, HISTORY_SLOTS + 1, jnp.int32)
    chosen = jax.random.randint(jax.random.fold_in(key, 1), (), 0, N_CTX, jnp.int32)
    return jnp.where(jnp.arange(N_CTX, dtype=jnp.int32) == chosen, HISTORY_SLOTS, counts).astype(jnp.int32)


def draw_head_groups(key, part):
    key = jax.random.fold_in(key, 15)
    order = jax.random.permutation(key, H)
    return (order // (H // KVH)).astype(jnp.int32)


def plant(result, stream_key, smallest, high):
    index_at = [jax.random.randint(jax.random.fold_in(stream_key, axis), (), 0, length) for axis, length in enumerate(result.shape)]
    main_axis = result.shape.index(max(result.shape))
    neighbour = index_at[:main_axis] + [(index_at[main_axis] + 1) % result.shape[main_axis]] + index_at[main_axis + 1:]
    return result.at[tuple(index_at)].set(smallest).at[tuple(neighbour)].set(high)


def strengthened(values, key, source, target, blocks, factor):
    owner, partner = [(jnp.arange(values.shape[axis_at]) // (values.shape[axis_at] // blocks)).reshape([-1 if axis == axis_at else 1 for axis in range(values.ndim)]) for axis_at in (source, target)]
    chosen = jax.random.permutation(key, blocks)[partner]
    strong = (owner == chosen) | (owner == (partner + blocks // 2) % blocks)
    return jnp.where(strong, factor * values, values)


def shard_levels(stream_key, shape, cuts, least, top_value):
    loudness, own = 1.0, jax.random.fold_in(stream_key, 6)
    for dim, shards_of in cuts:
        steps = jnp.exp(jax.random.uniform(jax.random.fold_in(own, dim), (shards_of,), jnp.float32, least / len(cuts), top_value / len(cuts)))
        loudness = loudness * jnp.repeat(steps, shape[dim] // shards_of).reshape([-1 if axis == dim else 1 for axis in range(len(shape))])
    return loudness


def normal_values(rng, dims, deviation, reach, cuts=(), kind=jnp.bfloat16):
    gain = shard_levels(rng, dims, cuts, -0.22, 0.18) if cuts else 1.0
    values = jax.random.normal(rng, dims, jnp.float32) * deviation * gain
    return jnp.minimum(jnp.maximum(values, -reach), reach).astype(kind)


def heavy_noise(own_key, dims, spread, reach, cuts, heavy, kind=jnp.bfloat16):
    drawn = spread * jax.random.normal(own_key, dims, jnp.float32)
    if cuts:
        drawn = drawn * shard_levels(own_key, dims, cuts, -0.22, 0.18)
    return jnp.clip(strengthened(drawn, jax.random.fold_in(own_key, 3), *heavy), -reach, reach).astype(kind)


def setup_inputs(seed: int = 0) -> dict:
    seeds = jax.random.split(jax.random.key(seed), 12)
    queries = draw_queries(jax.random.fold_in(seeds[11], 71), 0)
    cache_keys = draw_cache_keys(jax.random.fold_in(seeds[11], 71), 0)
    cache_values = normal_values(seeds[2], (KVH, SLOTS, DH), 1.0, 6.0, ((1, 8),))
    scale_index = plant(jax.random.randint(seeds[3], (KVH, NBLK), 0, NSCALE), jax.random.fold_in(seeds[3], 1), 0, NSCALE - 1).astype(jnp.int32)
    scale_table = jnp.clip(jnp.exp(jax.random.uniform(seeds[4], (2, NSCALE), jnp.float32, math.log(0.6), math.log(1.6))), 0.6, 1.6)
    hist_lengths = draw_hist_lengths(jax.random.fold_in(seeds[11], 71), 0)
    span_offsets = plant(jax.random.randint(seeds[6], (SPANS,), 0, SLOTS + 1), jax.random.fold_in(seeds[6], 1), 0, SLOTS).astype(jnp.int32)
    new_keys = draw_new_keys(jax.random.fold_in(seeds[11], 71), 0)
    new_values = normal_values(seeds[8], (QROWS, KVH, DH), 1.0, 6.0, ((0, 8),))
    head_groups = draw_head_groups(jax.random.fold_in(seeds[11], 71), 0)
    out_weight = heavy_noise(seeds[10], (H * DH, D_OUT), (H * DH // 64) ** -0.5, 0.75, ((0, 32),), (0, 1, 32, 2.75))
    return {"queries": queries, "cache_keys": cache_keys, "cache_values": cache_values, "scale_index": scale_index, "scale_table": scale_table, "hist_lengths": hist_lengths, "span_offsets": span_offsets, "new_keys": new_keys, "new_values": new_values, "head_groups": head_groups, "out_weight": out_weight}


floor_score = -1e+30

def reference(queries, cache_keys, cache_values, scale_index, scale_table, hist_lengths, span_offsets, new_keys, new_values, head_groups, out_weight):
    inverse = 1.0 / math.sqrt(DH)
    starts = (jnp.cumsum(hist_lengths) - hist_lengths).astype(jnp.int32)
    per_block_key_scales = jnp.repeat(scale_table[0][scale_index], SBLK, axis=1) * inverse
    value_scales = jnp.repeat(scale_table[1][scale_index], SBLK, axis=1)
    row_limits = jnp.repeat(span_offsets, SPAN)
    slot_ids = jnp.arange(HISTORY_SLOTS, dtype=jnp.int32)
    causal = jnp.arange(SPAN)[:, None] >= jnp.arange(SPAN)[None, :]

    def one_head(head):
        head_group_index = head_groups[head]
        query = queries[:, head, :]
        keys_all = cache_keys[head_group_index]
        values_all = cache_values[head_group_index]
        key_scale_factor = per_block_key_scales[head_group_index]
        vscale = value_scales[head_group_index]
        parts = []
        lses = []
        for block in range(N_CTX):
            leading_entry = block * HISTORY_SLOTS
            unscaled_scores = jnp.dot(query, keys_all[leading_entry:leading_entry + HISTORY_SLOTS].T, preferred_element_type=jnp.float32)
            logit_scores = unscaled_scores * key_scale_factor[leading_entry:leading_entry + HISTORY_SLOTS]
            live = slot_ids < hist_lengths[block]
            visible = live[None, :] & ((starts[block] + slot_ids)[None, :] < row_limits[:, None])
            masked = jnp.where(visible, logit_scores, floor_score)
            block_top = lax.optimization_barrier(jnp.max(masked, axis=1))
            block_expo = jnp.where(visible, jnp.exp(masked - block_top[:, None]), 0.0)
            any_visible = jnp.any(visible, axis=1)
            block_total = jnp.where(any_visible, lax.optimization_barrier(jnp.sum(block_expo, axis=1)), 1.0)
            weights = (block_expo * vscale[leading_entry:leading_entry + HISTORY_SLOTS]).astype(jnp.bfloat16)
            mixed = jnp.dot(weights, values_all[leading_entry:leading_entry + HISTORY_SLOTS], preferred_element_type=jnp.float32) / block_total[:, None]
            parts.append(mixed.astype(jnp.bfloat16))
            lses.append(jnp.where(any_visible, block_top + jnp.log(block_total), floor_score))
        query_spans = query.reshape(SPANS, SPAN, DH).astype(jnp.float32)
        key_spans = new_keys[:, head_group_index, :].reshape(SPANS, SPAN, DH).astype(jnp.float32)
        value_spans = new_values[:, head_group_index, :].reshape(SPANS, SPAN, DH).astype(jnp.float32)
        fresh_raw = jnp.einsum('crd,csd->crs', query_spans, key_spans) * inverse
        fresh_masked = jnp.where(causal[None], fresh_raw, floor_score)
        fresh_top = lax.optimization_barrier(jnp.max(fresh_masked, axis=2))
        fresh_expo = jnp.where(causal[None], jnp.exp(fresh_masked - fresh_top[:, :, None]), 0.0)
        fresh_total = lax.optimization_barrier(jnp.sum(fresh_expo, axis=2))
        fresh_weights = fresh_expo.astype(jnp.bfloat16).astype(jnp.float32)
        fresh = jnp.einsum('crs,csd->crd', fresh_weights, value_spans) / fresh_total[:, :, None]
        fresh = fresh.reshape(QROWS, DH)
        fresh_lse = (fresh_top + jnp.log(fresh_total)).reshape(QROWS)
        stacked = jnp.stack(lses)
        peak = jnp.maximum(lax.optimization_barrier(jnp.max(stacked, axis=0)), fresh_lse)
        block_weight = jnp.exp(stacked - peak[None, :])
        fresh_weight = jnp.exp(fresh_lse - peak)
        numer = fresh_weight[:, None] * fresh + lax.optimization_barrier(jnp.sum(block_weight[:, :, None] * jnp.stack(parts).astype(jnp.float32), axis=0))
        denom = fresh_weight + lax.optimization_barrier(jnp.sum(block_weight, axis=0))
        return (numer / denom[:, None]).astype(jnp.bfloat16)
    attended = lax.map(one_head, jnp.arange(H, dtype=jnp.int32))
    flat = jnp.transpose(attended, (1, 0, 2)).reshape(QROWS, H * DH)
    return jnp.dot(flat, out_weight, preferred_element_type=jnp.float32).astype(jnp.bfloat16)
```

```python
import functools
import math

import jax
import jax.numpy as jnp
from jax import lax
from jax.experimental import pallas as pl
from jax.experimental.pallas import tpu as pltpu
from jax.sharding import PartitionSpec as P

SPAN = 128
SBLK = 128
HEADS = 4
ROWS = 256
DH = 128
SLOTS = 768
BLOCKS = SLOTS // SBLK
PART_ROWS = HEADS * DH
LSE_ROWS = 32
MSG_ROWS = PART_ROWS + LSE_ROWS
FLOOR = -1e30
LOG2E = math.log2(math.e)
INVERSE = 1.0 / math.sqrt(DH)
AXES = ("ctx", "head")
F32, BF16, I32 = jnp.float32, jnp.bfloat16, jnp.int32
VMEM_LIMIT = 24 * 1024 * 1024
HPS = 2


def linear(y, xh, z, xl, core):
    return (((y % 4) * 2 + xh % 2) * 8 + z % 8) * 4 + (xl % 2) * 2 + core % 2


def moved(dy=0, dxh=0, dz=0, dxl=0, dcore=0):
    return [
        (linear(y, xh, z, xl, c), linear(y + dy, xh + dxh, z + dz, xl + dxl, c + dcore))
        for y in range(4)
        for xh in range(2)
        for z in range(8)
        for xl in range(2)
        for c in range(2)
    ]


def send(value, **move):
    return lax.ppermute(value, AXES, moved(**move))


def params():
    return pltpu.CompilerParams(vmem_limit_bytes=VMEM_LIMIT)


def log2(value):
    return jnp.log(value) * LOG2E


def pack_lse(lse8):
    high = lse8.astype(BF16).astype(F32)
    rest = lse8 - high
    middle = rest.astype(BF16).astype(F32)
    low = (rest - middle).astype(BF16).astype(F32)
    return jnp.concatenate([high, middle, low, jnp.zeros_like(low)], axis=0).astype(BF16)


def unpack_lse(packed):
    wide = packed.astype(F32)
    return wide[0:8] + wide[8:16] + wide[16:24]


def history_kernel(merge, groups, counts, scale_index, scale_table, *refs):
    q_ref = refs[0]
    k_refs = refs[1 : 1 + HPS]
    v_refs = refs[1 + HPS : 1 + 2 * HPS]
    rest = refs[1 + 2 * HPS :]
    if merge:
        prev_ref, prev_lse_ref, out_ref, lse_ref, weights_ref, held_ref = rest
    else:
        out_ref, lse_ref, weights_ref = rest
    step = pl.program_id(0)

    @pl.when(step == 0)
    def _():
        lse_ref[...] = jnp.full((8, ROWS), FLOOR, F32)
        if merge:
            held_ref[...] = unpack_lse(prev_lse_ref[...])

    lane = lax.broadcasted_iota(I32, (1, ROWS), 1)
    count = jnp.where(lane < SPAN, counts[0], counts[1])
    slot = lax.broadcasted_iota(I32, (SBLK, ROWS), 0)
    for local in range(HPS):
        head = step * HPS + local
        group = groups[head]
        query = q_ref[pl.ds(local * ROWS, ROWS), :]
        raw = lax.dot_general(
            k_refs[local][0], query, (((1,), (1,)), ((), ())), preferred_element_type=F32
        )
        scores = []
        for block in range(BLOCKS):
            scale = scale_table[0, scale_index[group, block]] * (INVERSE * LOG2E)
            piece = raw[block * SBLK : (block + 1) * SBLK] * scale
            scores.append(jnp.where(slot < count - block * SBLK, piece, FLOOR))
        top = functools.reduce(jnp.maximum, scores)
        top = jnp.max(top, axis=0, keepdims=True)
        total = jnp.zeros((SBLK, ROWS), F32)
        for block in range(BLOCKS):
            scale = scale_table[1, scale_index[group, block]]
            expo = jnp.exp2(scores[block] - top)
            total = total + expo
            weights_ref[local, block * SBLK : (block + 1) * SBLK, :] = (expo * scale).astype(BF16)
        total = jnp.sum(total, axis=0, keepdims=True)
        mixed = jnp.dot(v_refs[local][0], weights_ref[local], preferred_element_type=F32)
        seen = count > 0
        lse = jnp.where(seen, top + log2(total), FLOOR)
        share = jnp.where(seen, 1.0 / total, 0.0)
        rows = pl.ds(local * DH, DH)
        if merge:
            before = held_ref[pl.ds(head, 1), :]
            peak = jnp.maximum(lse, before)
            mine = jnp.exp2(lse - peak)
            other = jnp.exp2(before - peak)
            both = mine + other
            inverse = 1.0 / both
            mixed = mixed * (share * mine * inverse)
            mixed = mixed + prev_ref[rows, :].astype(F32) * (other * inverse)
            lse = peak + log2(both)
        else:
            mixed = mixed * share
        out_ref[pl.ds(pl.multiple_of(head * DH, DH), DH), :] = mixed.astype(BF16)
        lse_ref[pl.ds(head, 1), :] = lse

    @pl.when(step == HEADS // HPS - 1)
    def _():
        out_ref[PART_ROWS:, :] = pack_lse(lse_ref[...])


def history(groups, counts, scale_index, scale_table, query, keys, values_t, previous=None):
    merge = previous is not None

    def of_group(local):
        return lambda i, g, *_: (g[i * HPS + local], 0, 0)

    in_specs = [pl.BlockSpec((HPS * ROWS, DH), lambda i, *_: (i, 0))]
    in_specs += [pl.BlockSpec((1, SLOTS, DH), of_group(local)) for local in range(HPS)]
    in_specs += [pl.BlockSpec((1, DH, SLOTS), of_group(local)) for local in range(HPS)]
    operands = [query] + [keys] * HPS + [values_t] * HPS
    scratch = [pltpu.VMEM((8, ROWS), F32), pltpu.VMEM((HPS, SLOTS, ROWS), BF16)]
    if merge:
        in_specs += [
            pl.BlockSpec((HPS * DH, ROWS), lambda i, *_: (i, 0)),
            pl.BlockSpec((LSE_ROWS, ROWS), lambda i, *_: (PART_ROWS // LSE_ROWS, 0)),
        ]
        operands += [previous, previous]
        scratch += [pltpu.VMEM((8, ROWS), F32)]
    return pl.pallas_call(
        functools.partial(history_kernel, merge),
        out_shape=jax.ShapeDtypeStruct((MSG_ROWS, ROWS), BF16),
        grid_spec=pltpu.PrefetchScalarGridSpec(
            num_scalar_prefetch=4,
            grid=(HEADS // HPS,),
            in_specs=in_specs,
            out_specs=pl.BlockSpec((MSG_ROWS, ROWS), lambda i, *_: (0, 0)),
            scratch_shapes=scratch,
        ),
        compiler_params=params(),
        cost_estimate=pl.CostEstimate(
            flops=4 * HEADS * ROWS * SLOTS * DH,
            bytes_accessed=2 * HEADS * SLOTS * DH * 2,
            transcendentals=HEADS * ROWS * SLOTS,
        ),
    )(groups, counts, scale_index, scale_table, *operands)


def fresh_kernel(groups, q_ref, k_ref, v_ref, out_ref, lse_ref):
    head = pl.program_id(0)

    @pl.when(head == 0)
    def _():
        lse_ref[...] = jnp.zeros((8, ROWS), F32)

    raw = lax.dot_general(
        k_ref[0], q_ref[...], (((1,), (1,)), ((), ())), preferred_element_type=F32
    )
    column = lax.broadcasted_iota(I32, (ROWS, ROWS), 0)
    row = lax.broadcasted_iota(I32, (ROWS, ROWS), 1)
    visible = (column <= row) & ((column >= SPAN) | (row < SPAN))
    score = jnp.where(visible, raw * (INVERSE * LOG2E), FLOOR)
    top = jnp.max(score, axis=0, keepdims=True)
    expo = jnp.exp2(score - top)
    total = jnp.sum(expo, axis=0, keepdims=True)
    mixed = jnp.dot(v_ref[0], expo.astype(BF16), preferred_element_type=F32)
    out_ref[...] = mixed * (1.0 / total)
    lse_ref[pl.ds(head, 1), :] = top + log2(total)


def fresh_part(groups, query, new_keys, new_values_t):
    return pl.pallas_call(
        fresh_kernel,
        out_shape=(
            jax.ShapeDtypeStruct((PART_ROWS, ROWS), F32),
            jax.ShapeDtypeStruct((8, ROWS), F32),
        ),
        grid_spec=pltpu.PrefetchScalarGridSpec(
            num_scalar_prefetch=1,
            grid=(HEADS,),
            in_specs=[
                pl.BlockSpec((ROWS, DH), lambda i, *_: (i, 0)),
                pl.BlockSpec((1, ROWS, DH), lambda i, g: (g[i], 0, 0)),
                pl.BlockSpec((1, DH, ROWS), lambda i, g: (g[i], 0, 0)),
            ],
            out_specs=(
                pl.BlockSpec((DH, ROWS), lambda i, *_: (i, 0)),
                pl.BlockSpec((8, ROWS), lambda i, *_: (0, 0)),
            ),
        ),
        compiler_params=params(),
        cost_estimate=pl.CostEstimate(
            flops=4 * HEADS * ROWS * ROWS * DH,
            bytes_accessed=HEADS * ROWS * DH * 6,
            transcendentals=HEADS * ROWS * ROWS,
        ),
    )(groups, query, new_keys, new_values_t)


def combine_kernel(a_ref, b_ref, c_ref, d_ref, fresh_ref, fresh_lse_ref, out_ref):
    parts = (a_ref, b_ref, c_ref, d_ref)
    lses = [unpack_lse(part[PART_ROWS:, :]) for part in parts]
    fresh_lse = fresh_lse_ref[...]
    peak = functools.reduce(jnp.maximum, lses, fresh_lse)
    weights = [jnp.exp2(lse - peak) for lse in lses]
    fresh_weight = jnp.exp2(fresh_lse - peak)
    inverse = 1.0 / functools.reduce(jnp.add, weights, fresh_weight)
    weights = [weight * inverse for weight in weights]
    fresh_weight = fresh_weight * inverse
    for head in range(HEADS):
        rows = slice(head * DH, (head + 1) * DH)
        total = fresh_ref[rows, :] * fresh_weight[head : head + 1]
        for part, weight in zip(parts, weights):
            total = total + part[rows, :].astype(F32) * weight[head : head + 1]
        out_ref[:, rows] = jnp.transpose(total).astype(BF16)


def combined(parts, fresh, fresh_lse):
    return pl.pallas_call(
        combine_kernel,
        out_shape=jax.ShapeDtypeStruct((ROWS, PART_ROWS), BF16),
        in_specs=[pl.BlockSpec(memory_space=pltpu.VMEM)] * 6,
        out_specs=pl.BlockSpec(memory_space=pltpu.VMEM),
        compiler_params=params(),
        cost_estimate=pl.CostEstimate(
            flops=10 * ROWS * PART_ROWS, bytes_accessed=3 * 2**20, transcendentals=0
        ),
    )(*parts, fresh, fresh_lse)


def copy_kernel(core, w_ref, out_ref):
    out_ref[0] = w_ref[...]


def columns_of(core, weight):
    depth, width = weight.shape
    count = width // (2 * ROWS)
    return pl.pallas_call(
        copy_kernel,
        out_shape=jax.ShapeDtypeStruct((count, depth, ROWS), BF16),
        grid_spec=pltpu.PrefetchScalarGridSpec(
            num_scalar_prefetch=1,
            grid=(count,),
            in_specs=[pl.BlockSpec((depth, ROWS), lambda i, c: (0, 2 * i + c[0]))],
            out_specs=pl.BlockSpec((1, depth, ROWS), lambda i, c: (i, 0, 0)),
        ),
        compiler_params=params(),
        cost_estimate=pl.CostEstimate(
            flops=0, bytes_accessed=2 * depth * width, transcendentals=0
        ),
    )(core, weight)


def project_kernel(own_at, other_at, a_ref, b_ref, w_ref, v_ref, out_ref):
    total = jnp.dot(a_ref[...], w_ref[...], preferred_element_type=F32)
    total = total + jnp.dot(b_ref[...], v_ref[0], preferred_element_type=F32)
    out_ref[0] = total.astype(out_ref.dtype)


def projected(own_at, other_at, mine, theirs, weight, other_weight, kind):
    count = own_at.shape[0]
    depth = weight.shape[0]
    return pl.pallas_call(
        project_kernel,
        out_shape=jax.ShapeDtypeStruct((count, ROWS, ROWS), kind),
        grid_spec=pltpu.PrefetchScalarGridSpec(
            num_scalar_prefetch=2,
            grid=(count,),
            in_specs=[
                pl.BlockSpec((ROWS, depth), lambda i, *_: (0, 0)),
                pl.BlockSpec((ROWS, depth), lambda i, *_: (0, 0)),
                pl.BlockSpec((depth, ROWS), lambda i, a, b: (0, a[i])),
                pl.BlockSpec((1, depth, ROWS), lambda i, a, b: (b[i], 0, 0)),
            ],
            out_specs=pl.BlockSpec((1, ROWS, ROWS), lambda i, *_: (i, 0, 0)),
        ),
        compiler_params=params(),
        cost_estimate=pl.CostEstimate(
            flops=count * 4 * ROWS * ROWS * depth,
            bytes_accessed=count * 4 * ROWS * depth,
            transcendentals=0,
        ),
    )(own_at, other_at, mine, theirs, weight, other_weight)


def shards(
    queries,
    cache_keys,
    cache_values,
    scale_index,
    scale_table,
    hist_lengths,
    span_offsets,
    new_keys,
    new_values,
    head_groups,
    out_weight,
):
    ctx, place = lax.axis_index("ctx"), lax.axis_index("head")
    y, xh = ctx // 2, ctx % 2
    z, xl, core = place // 4, (place // 2) % 2, place % 2

    q0 = jnp.transpose(queries, (1, 0, 2)).reshape(HEADS * ROWS, DH)
    p0 = send(q0, dxh=1, dxl=1)
    q_down = send(q0, dy=1)
    q_up = send(q0, dy=-1)

    small = jnp.concatenate([head_groups, hist_lengths])
    small_pair = send(small, dxh=1, dxl=1)
    pair_groups = small_pair[:HEADS]
    pair_length = small_pair[HEADS:]
    both = hist_lengths + pair_length
    start = jnp.where(xh == 1, pair_length, 0)
    for step in (1, -1, 2):
        start = start + jnp.where((y - step) % 4 < y, send(both, dy=step), 0)
    start = start[0]
    length = hist_lengths[0]

    def counts(source_y, source_xh):
        source = (source_y % 4) * 2 + source_xh
        offsets = lax.dynamic_slice_in_dim(span_offsets, source * 2, 2)
        return jnp.clip(jnp.minimum(length, offsets - start), 0, SLOTS)

    q_far = send(q0, dy=2)
    p_down = send(p0, dy=1)
    p_up = send(p0, dy=-1)
    p_far = send(q_far, dxh=1, dxl=1)

    other_weight = send(columns_of((1 - core)[None], out_weight), dcore=1)
    values_t = jnp.swapaxes(cache_values, 1, 2)
    fresh, fresh_lse = fresh_part(
        head_groups,
        q0,
        jnp.transpose(new_keys, (1, 0, 2)),
        jnp.transpose(new_values, (1, 2, 0)),
    )

    def attend(groups, source_y, source_xh, query, previous=None):
        return history(
            groups,
            counts(source_y, source_xh),
            scale_index,
            scale_table,
            query,
            cache_keys,
            values_t,
            previous,
        )

    back = {}
    for step, query in ((0, p0), (-1, p_down), (1, p_up), (2, p_far)):
        back[step] = send(attend(pair_groups, y + step, 1 - xh, query), dxh=1, dxl=1)
    parts = []
    for step, query in ((0, q0), (-1, q_down), (1, q_up), (2, q_far)):
        part = attend(head_groups, y + step, xh, query, back[step])
        parts.append(send(part, dy=step) if step else part)

    mine = combined(parts, fresh, fresh_lse)
    theirs = send(mine, dcore=1)

    def project(steps, kind=F32):
        at = jnp.stack([((z + step) % 8) * 2 + xl ^ other for step, other in steps])
        return projected(2 * at + core, at, mine, theirs, out_weight, other_weight, kind)

    first = project([(4, 0), (4, 1)], BF16)
    up = send(first[0:1], dz=1)
    down = send(first[1:2], dz=-1)
    for step in (3, 2, 1):
        partial = project([(step, 0), (step, 1), (-step, 0), (-step, 1)])
        if step == 3:
            up = jnp.concatenate([partial[0:1] + up.astype(F32), partial[1:2]])
            down = jnp.concatenate([partial[2:3], partial[3:4] + down.astype(F32)])
        else:
            up = partial[0:2] + up.astype(F32)
            down = partial[2:4] + down.astype(F32)
        up = send(up.astype(BF16), dz=1)
        down = send(down.astype(BF16), dz=-1)
    partial = project([(0, 0), (0, 1)])
    total = partial + up.astype(F32) + down.astype(F32)
    across = send(total[1].astype(BF16), dxl=1)
    return (total[0] + across.astype(F32)).astype(BF16)


def solution(mesh):
    placed = (
        P("ctx", "head", None),
        P(None, "ctx", None),
        P(None, "ctx", None),
        P(None, "ctx"),
        P(),
        P("ctx"),
        P(),
        P("ctx", None, None),
        P("ctx", None, None),
        P("head"),
        P("head", None),
    )
    return jax.shard_map(
        shards, mesh=mesh, in_specs=placed, out_specs=P("ctx", "head"), check_vma=False
    )
```

```python
import functools
import math

import jax
import jax.numpy as jnp
from jax import lax
from jax.experimental import pallas as pl
from jax.experimental.pallas import tpu as pltpu
from jax.sharding import PartitionSpec as P

SPAN = 128
SBLK = 128
HEADS = 4
ROWS = 256
DH = 128
SLOTS = 768
BLOCKS = SLOTS // SBLK
PART_ROWS = HEADS * DH
LSE_ROWS = 32
MSG_ROWS = PART_ROWS + LSE_ROWS
FLOOR = -1e30
LOG2E = math.log2(math.e)
INVERSE = 1.0 / math.sqrt(DH)
AXES = ("ctx", "head")
F32, BF16, I32 = jnp.float32, jnp.bfloat16, jnp.int32
VMEM_LIMIT = 20 * 1024 * 1024


def linear(y, xh, z, xl, core):
    return (((y % 4) * 2 + xh % 2) * 8 + z % 8) * 4 + (xl % 2) * 2 + core % 2


def moved(dy=0, dxh=0, dz=0, dxl=0, dcore=0):
    return [
        (linear(y, xh, z, xl, c), linear(y + dy, xh + dxh, z + dz, xl + dxl, c + dcore))
        for y in range(4)
        for xh in range(2)
        for z in range(8)
        for xl in range(2)
        for c in range(2)
    ]


def send(value, **move):
    return lax.ppermute(value, AXES, moved(**move))


def params():
    return pltpu.CompilerParams(vmem_limit_bytes=VMEM_LIMIT)


def fixed(value, space=pltpu.VMEM):
    return pltpu.with_memory_space_constraint(value, space)


def log2(value):
    return jnp.log(value) * LOG2E


def pack_lse(lse8):
    high = lse8.astype(BF16).astype(F32)
    rest = lse8 - high
    middle = rest.astype(BF16).astype(F32)
    low = (rest - middle).astype(BF16).astype(F32)
    return jnp.concatenate([high, middle, low, jnp.zeros_like(low)], axis=0).astype(BF16)


def unpack_lse(packed):
    wide = packed.astype(F32)
    return wide[0:8] + wide[8:16] + wide[16:24]


def history_kernel(blocks, at, groups, counts, scale_index, scale_table, *refs):
    q_refs, (k_ref, v_ref, *rest) = refs[:blocks], refs[blocks:]
    if at is not None:
        prev_ref, out_ref, weights_ref = rest
    else:
        out_ref, weights_ref = rest
    lane = lax.broadcasted_iota(I32, (1, ROWS), 1)
    slot = lax.broadcasted_iota(I32, (SBLK, ROWS), 0)
    units = [(block, head) for block in range(blocks) for head in range(HEADS)]

    def products(unit):
        block, head = units[unit]
        return lax.dot_general(
            k_ref[groups[head]],
            q_refs[block][head * ROWS : (head + 1) * ROWS, :],
            (((1,), (1,)), ((), ())),
            preferred_element_type=F32,
        )

    following = products(0)
    for unit, (block, head) in enumerate(units):
        if head == 0:
            lses = []
            count = jnp.where(lane < SPAN, counts[2 * block], counts[2 * block + 1])
            seen = count > 0
            if at is not None:
                held = unpack_lse(prev_ref[at, PART_ROWS:, :])
        group = groups[head]
        raw = following
        if unit + 1 < len(units):
            following = products(unit + 1)
        scores = []
        for part in range(BLOCKS):
            scale = scale_table[0, scale_index[group, part]] * (INVERSE * LOG2E)
            piece = raw[part * SBLK : (part + 1) * SBLK] * scale
            scores.append(jnp.where(slot < count - part * SBLK, piece, FLOOR))
        top = functools.reduce(jnp.maximum, scores)
        top = jnp.max(top, axis=0, keepdims=True)
        total = jnp.zeros((SBLK, ROWS), F32)
        for part in range(BLOCKS):
            scale = scale_table[1, scale_index[group, part]]
            expo = jnp.exp2(scores[part] - top)
            total = total + expo
            weights_ref[head, part * SBLK : (part + 1) * SBLK, :] = (expo * scale).astype(BF16)
        total = jnp.sum(total, axis=0, keepdims=True)
        mixed = times_transposed(v_ref[group], weights_ref[head])
        lse = jnp.where(seen, top + log2(total), FLOOR)
        share = jnp.where(seen, 1.0 / total, 0.0)
        rows = slice(head * DH, (head + 1) * DH)
        if at is not None:
            before = held[head : head + 1]
            peak = jnp.maximum(lse, before)
            mine = jnp.exp2(lse - peak)
            other = jnp.exp2(before - peak)
            both = mine + other
            inverse = 1.0 / both
            mixed = mixed * (share * mine * inverse)
            mixed = mixed + prev_ref[at, rows, :].astype(F32) * (other * inverse)
            lse = peak + log2(both)
        else:
            mixed = mixed * share
        out_ref[block, rows, :] = mixed.astype(BF16)
        lses.append(lse)
        if head == HEADS - 1:
            lses.append(jnp.zeros((8 - HEADS, ROWS), F32))
            out_ref[block, PART_ROWS:, :] = pack_lse(jnp.concatenate(lses, axis=0))


def times_transposed(values, weights):
    return lax.dot_general(
        values, weights, (((0,), (0,)), ((), ())), preferred_element_type=F32
    )


def in_vmem():
    return pl.BlockSpec(memory_space=pltpu.VMEM)


def in_smem():
    return pl.BlockSpec(memory_space=pltpu.SMEM)


def history(groups, counts, scale_index, scale_table, queries, keys, values, previous=None):
    blocks = len(queries)
    operands = [*queries, keys, values]
    at = None
    if previous is not None:
        held, at = previous
        operands.append(held)
    return pl.pallas_call(
        functools.partial(history_kernel, blocks, at),
        out_shape=jax.ShapeDtypeStruct((blocks, MSG_ROWS, ROWS), BF16),
        in_specs=[in_smem()] * 4 + [in_vmem()] * len(operands),
        out_specs=in_vmem(),
        scratch_shapes=[pltpu.VMEM((HEADS, SLOTS, ROWS), BF16)],
        compiler_params=params(),
        cost_estimate=pl.CostEstimate(
            flops=4 * blocks * HEADS * ROWS * SLOTS * DH,
            bytes_accessed=2 * HEADS * SLOTS * DH * 2,
            transcendentals=blocks * HEADS * ROWS * SLOTS,
        ),
    )(groups, counts, scale_index, scale_table, *operands)


def fresh_kernel(groups, q_ref, k_ref, v_ref, out_ref, lse_ref):
    column = lax.broadcasted_iota(I32, (ROWS, ROWS), 0)
    row = lax.broadcasted_iota(I32, (ROWS, ROWS), 1)
    visible = (column <= row) & ((column >= SPAN) | (row < SPAN))
    lses = []
    for head in range(HEADS):
        group = groups[head]
        raw = lax.dot_general(
            k_ref[group],
            q_ref[head * ROWS : (head + 1) * ROWS, :],
            (((1,), (1,)), ((), ())),
            preferred_element_type=F32,
        )
        score = jnp.where(visible, raw * (INVERSE * LOG2E), FLOOR)
        top = jnp.max(score, axis=0, keepdims=True)
        expo = jnp.exp2(score - top)
        total = jnp.sum(expo, axis=0, keepdims=True)
        mixed = times_transposed(v_ref[group], expo.astype(BF16))
        out_ref[head * DH : (head + 1) * DH, :] = mixed * (1.0 / total)
        lses.append(top + log2(total))
    lses.append(jnp.zeros((8 - HEADS, ROWS), F32))
    lse_ref[...] = jnp.concatenate(lses, axis=0)


def fresh_part(groups, query, new_keys, new_values):
    return pl.pallas_call(
        fresh_kernel,
        out_shape=(
            jax.ShapeDtypeStruct((PART_ROWS, ROWS), F32),
            jax.ShapeDtypeStruct((8, ROWS), F32),
        ),
        in_specs=[in_smem()] + [in_vmem()] * 3,
        out_specs=(in_vmem(), in_vmem()),
        compiler_params=params(),
        cost_estimate=pl.CostEstimate(
            flops=4 * HEADS * ROWS * ROWS * DH,
            bytes_accessed=HEADS * ROWS * DH * 6,
            transcendentals=HEADS * ROWS * ROWS,
        ),
    )(groups, query, new_keys, new_values)


def combine_kernel(a_ref, b_ref, c_ref, d_ref, fresh_ref, fresh_lse_ref, out_ref):
    parts = (a_ref, b_ref, c_ref, d_ref)
    lses = [unpack_lse(part[0, PART_ROWS:, :]) for part in parts]
    fresh_lse = fresh_lse_ref[...]
    peak = functools.reduce(jnp.maximum, lses, fresh_lse)
    weights = [jnp.exp2(lse - peak) for lse in lses]
    fresh_weight = jnp.exp2(fresh_lse - peak)
    inverse = 1.0 / functools.reduce(jnp.add, weights, fresh_weight)
    weights = [weight * inverse for weight in weights]
    fresh_weight = fresh_weight * inverse
    for head in range(HEADS):
        rows = slice(head * DH, (head + 1) * DH)
        total = fresh_ref[rows, :] * fresh_weight[head : head + 1]
        for part, weight in zip(parts, weights):
            total = total + part[0, rows, :].astype(F32) * weight[head : head + 1]
        out_ref[:, rows] = jnp.transpose(total).astype(BF16)


def combined(parts, fresh, fresh_lse):
    return pl.pallas_call(
        combine_kernel,
        out_shape=jax.ShapeDtypeStruct((ROWS, PART_ROWS), BF16),
        in_specs=[pl.BlockSpec(memory_space=pltpu.VMEM)] * 6,
        out_specs=pl.BlockSpec(memory_space=pltpu.VMEM),
        compiler_params=params(),
        cost_estimate=pl.CostEstimate(
            flops=10 * ROWS * PART_ROWS, bytes_accessed=3 * 2**20, transcendentals=0
        ),
    )(*parts, fresh, fresh_lse)


def load_kernel(core, *refs):
    (*whole_in, weight), outs, sems = refs[: len(refs) // 2], refs[len(refs) // 2 : -1], refs[-1]
    pairs = []
    for source, target in zip(whole_in, outs):
        for group in range(source.shape[0]):
            pairs.append((source.at[group], target.at[group]))
    for block in range(outs[-1].shape[0]):
        columns = pl.ds(pl.multiple_of((2 * block + core[0]) * ROWS, ROWS), ROWS)
        pairs.append((weight.at[:, columns], outs[-1].at[block]))
    copies = [
        pltpu.make_async_copy(source, target, sems.at[place])
        for place, (source, target) in enumerate(pairs)
    ]
    for copy in copies:
        copy.start()
    for copy in copies:
        copy.wait()


def loaded(core, weight, *whole):
    depth, width = weight.shape
    count = width // (2 * ROWS)
    shapes = [value.shape for value in whole] + [(count, depth, ROWS)]
    total = count + sum(value.shape[0] for value in whole)
    return pl.pallas_call(
        load_kernel,
        out_shape=[pltpu.VMEM(shape, BF16) for shape in shapes],
        in_specs=[in_smem()] + [pl.BlockSpec(memory_space=pltpu.HBM)] * len(shapes),
        out_specs=[in_vmem()] * len(shapes),
        scratch_shapes=[pltpu.SemaphoreType.DMA((total,))],
        compiler_params=params(),
        cost_estimate=pl.CostEstimate(
            flops=0, bytes_accessed=2 * depth * width, transcendentals=0
        ),
    )(core, *[fixed(value, pltpu.HBM) for value in (*whole, weight)])


def project_kernel(at, a_ref, b_ref, w_ref, v_ref, out_ref):
    for block in range(out_ref.shape[0]):
        total = jnp.dot(a_ref[...], w_ref[at[block]], preferred_element_type=F32)
        total = total + jnp.dot(b_ref[...], v_ref[at[block]], preferred_element_type=F32)
        out_ref[block] = total.astype(out_ref.dtype)


def projected(at, mine, theirs, weight, other_weight, kind):
    count = at.shape[0]
    depth = weight.shape[1]
    return pl.pallas_call(
        project_kernel,
        out_shape=jax.ShapeDtypeStruct((count, ROWS, ROWS), kind),
        in_specs=[in_smem()] + [in_vmem()] * 4,
        out_specs=in_vmem(),
        compiler_params=params(),
        cost_estimate=pl.CostEstimate(
            flops=count * 4 * ROWS * ROWS * depth,
            bytes_accessed=count * 4 * ROWS * depth,
            transcendentals=0,
        ),
    )(at, mine, theirs, fixed(weight), fixed(other_weight))


def shards(
    queries,
    cache_keys,
    cache_values,
    scale_index,
    scale_table,
    hist_lengths,
    span_offsets,
    new_keys,
    new_values,
    head_groups,
    out_weight,
):
    ctx, place = lax.axis_index("ctx"), lax.axis_index("head")
    y, xh = ctx // 2, ctx % 2
    z, xl, core = place // 4, (place // 2) % 2, place % 2

    q0 = jnp.transpose(queries, (1, 0, 2)).reshape(HEADS * ROWS, DH)
    p0 = send(q0, dxh=1, dxl=1)
    q_down = send(q0, dy=1)
    q_up = send(q0, dy=-1)
    pair_groups = send(head_groups, dxh=1, dxl=1)
    lengths = lax.all_to_all(
        jnp.broadcast_to(hist_lengths, (8,)), "ctx", split_axis=0, concat_axis=0, tiled=True
    )
    sent_weight = send(out_weight, dcore=1)
    keys, values, weight = loaded(core[None], out_weight, cache_keys, cache_values)
    start = jnp.sum(jnp.where(jnp.arange(8) < ctx, lengths, 0))
    length = hist_lengths[0]
    p0, q_down, q_up, start, pair_groups, weight = lax.optimization_barrier(
        (p0, q_down, q_up, start, pair_groups, weight)
    )
    q_far = send(q0, dy=2)
    p_down = send(p0, dy=1)
    p_up = send(p0, dy=-1)
    p_far = send(q_far, dxh=1, dxl=1)

    def counts(source_y, source_xh):
        source = (source_y % 4) * 2 + source_xh
        offsets = lax.dynamic_slice_in_dim(span_offsets, source * 2, 2)
        return jnp.clip(jnp.minimum(length, offsets - start), 0, SLOTS)

    def attend(groups, sources, source_xh, queries, previous=None):
        return history(
            groups,
            jnp.concatenate([counts(y + step, source_xh) for step in sources]),
            scale_index,
            scale_table,
            queries,
            keys,
            values,
            previous,
        )

    first = attend(pair_groups, (0,), 1 - xh, [p0])
    back = {0: (send(first, dxh=1, dxl=1), 0)}
    fresh_keys, fresh_values, first = lax.optimization_barrier((new_keys, new_values, first))
    fresh, fresh_lse = fresh_part(
        head_groups,
        q0,
        jnp.transpose(fresh_keys, (1, 0, 2)),
        jnp.transpose(fresh_values, (1, 0, 2)),
    )
    p_down, p_up, p_far, fresh_lse = lax.optimization_barrier((p_down, p_up, p_far, fresh_lse))
    for step, query in ((-1, p_down), (1, p_up), (2, p_far)):
        back[step] = (send(attend(pair_groups, (step,), 1 - xh, [query]), dxh=1, dxl=1), 0)
    parts = []
    for step, query in ((0, q0), (-1, q_down), (1, q_up), (2, q_far)):
        part = attend(head_groups, (step,), xh, [query], back[step])
        parts.append(send(part, dy=step) if step else part)
    sent_weight, _ = lax.optimization_barrier((sent_weight, parts[0]))
    (other_weight,) = loaded(core[None], sent_weight)

    mine = combined(parts, fresh, fresh_lse)
    theirs = send(mine, dcore=1)

    def project(steps, kind, after=None):
        at = jnp.stack([(((z + step) % 8) * 2 + xl) ^ other for step, other in steps])
        if after is not None:
            at, _ = lax.optimization_barrier((at, after))
        return projected(at, mine, theirs, weight, other_weight, kind)

    first = project([(4, 0), (4, 1)], BF16)
    up = send(first[0:1], dz=1)
    down = send(first[1:2], dz=-1)
    whole = project(
        [(step, other) for step in (3, -3, 2, -2, 1, -1, 0) for other in (0, 1)], F32, first
    )
    for step in (3, 2, 1):
        partial = whole[4 * (3 - step) : 4 * (4 - step)]
        if step == 3:
            up = jnp.concatenate([partial[0:1] + up.astype(F32), partial[1:2]])
            down = jnp.concatenate([partial[2:3], partial[3:4] + down.astype(F32)])
        else:
            up = partial[0:2] + up.astype(F32)
            down = partial[2:4] + down.astype(F32)
        up = send(up.astype(BF16), dz=1)
        down = send(down.astype(BF16), dz=-1)
    total = whole[12:14] + up.astype(F32) + down.astype(F32)
    across = send(total[1].astype(BF16), dxl=1)
    return (total[0] + across.astype(F32)).astype(BF16)


def solution(mesh):
    placed = (
        P("ctx", "head", None),
        P(None, "ctx", None),
        P(None, "ctx", None),
        P(None, "ctx"),
        P(),
        P("ctx"),
        P(),
        P("ctx", None, None),
        P("ctx", None, None),
        P("head"),
        P("head", None),
    )
    return jax.shard_map(
        shards, mesh=mesh, in_specs=placed, out_specs=P("ctx", "head"), check_vma=False
    )
```

```python
import functools
import math

import jax
import jax.numpy as jnp
from jax import lax
from jax.experimental import pallas as pl
from jax.experimental.pallas import tpu as pltpu
from jax.sharding import PartitionSpec as P

SPAN = 128
SBLK = 128
HEADS = 4
ROWS = 256
DH = 128
SLOTS = 768
BLOCKS = SLOTS // SBLK
PART_ROWS = HEADS * DH
LSE_ROWS = 32
FACT_ROWS = 16
MSG_ROWS = PART_ROWS + LSE_ROWS
FLOOR = -1e30
LOG2E = math.log2(math.e)
INVERSE = 1.0 / math.sqrt(DH)
AXES = ("ctx", "head")
F32, BF16, I32 = jnp.float32, jnp.bfloat16, jnp.int32
VMEM_LIMIT = 20 * 1024 * 1024


def linear(y, xh, z, xl, core):
    return (((y % 4) * 2 + xh % 2) * 8 + z % 8) * 4 + (xl % 2) * 2 + core % 2


def moved(dy=0, dxh=0, dz=0, dxl=0, dcore=0):
    return [
        (linear(y, xh, z, xl, c), linear(y + dy, xh + dxh, z + dz, xl + dxl, c + dcore))
        for y in range(4)
        for xh in range(2)
        for z in range(8)
        for xl in range(2)
        for c in range(2)
    ]


def send(value, **move):
    return lax.ppermute(value, AXES, moved(**move))


def params():
    return pltpu.CompilerParams(vmem_limit_bytes=VMEM_LIMIT)


def fixed(value, space=pltpu.VMEM):
    return pltpu.with_memory_space_constraint(value, space)


def log2(value):
    return jnp.log(value) * LOG2E


def pack_lse(lse8):
    high = lse8.astype(BF16).astype(F32)
    rest = lse8 - high
    middle = rest.astype(BF16).astype(F32)
    low = (rest - middle).astype(BF16).astype(F32)
    return jnp.concatenate([high, middle, low, jnp.zeros_like(low)], axis=0).astype(BF16)


def unpack_lse(packed):
    wide = packed.astype(F32)
    return wide[0:8] + wide[8:16] + wide[16:24]


def history_kernel(blocks, at, later, groups, counts, scale_index, scale_table, *refs):
    refs = refs[later:]
    q_refs, (k_ref, v_ref, *rest) = refs[:blocks], refs[blocks:]
    if at is not None:
        prev_ref, out_ref, weights_ref = rest
    else:
        out_ref, weights_ref = rest
    lane = lax.broadcasted_iota(I32, (1, ROWS), 1)
    slot = lax.broadcasted_iota(I32, (SBLK, ROWS), 0)
    units = [(block, head) for block in range(blocks) for head in range(HEADS)]

    def products(unit):
        block, head = units[unit]
        return lax.dot_general(
            k_ref[groups[head]],
            q_refs[block][head * ROWS : (head + 1) * ROWS, :],
            (((1,), (1,)), ((), ())),
            preferred_element_type=F32,
        )

    following = products(0)
    for unit, (block, head) in enumerate(units):
        if head == 0:
            lses = []
            count = jnp.where(lane < SPAN, counts[2 * block], counts[2 * block + 1])
            seen = count > 0
            if at is not None:
                held = unpack_lse(prev_ref[at, PART_ROWS:, :])
        group = groups[head]
        raw = following
        if unit + 1 < len(units):
            following = products(unit + 1)
        scores = []
        for part in range(BLOCKS):
            scale = scale_table[0, scale_index[group, part]] * (INVERSE * LOG2E)
            piece = raw[part * SBLK : (part + 1) * SBLK] * scale
            scores.append(jnp.where(slot < count - part * SBLK, piece, FLOOR))
        top = functools.reduce(jnp.maximum, scores)
        top = jnp.max(top, axis=0, keepdims=True)
        total = jnp.zeros((SBLK, ROWS), F32)
        for part in range(BLOCKS):
            scale = scale_table[1, scale_index[group, part]]
            expo = jnp.exp2(scores[part] - top)
            total = total + expo
            weights_ref[head, part * SBLK : (part + 1) * SBLK, :] = (expo * scale).astype(BF16)
        total = jnp.sum(total, axis=0, keepdims=True)
        mixed = times_transposed(v_ref[group], weights_ref[head])
        lse = jnp.where(seen, top + log2(total), FLOOR)
        share = jnp.where(seen, 1.0 / total, 0.0)
        rows = slice(head * DH, (head + 1) * DH)
        if at is not None:
            before = held[head : head + 1]
            peak = jnp.maximum(lse, before)
            mine = jnp.exp2(lse - peak)
            other = jnp.exp2(before - peak)
            both = mine + other
            inverse = 1.0 / both
            mixed = mixed * (share * mine * inverse)
            mixed = mixed + prev_ref[at, rows, :].astype(F32) * (other * inverse)
            lse = peak + log2(both)
        else:
            mixed = mixed * share
        out_ref[block, rows, :] = mixed.astype(BF16)
        lses.append(lse)
        if head == HEADS - 1:
            lses.append(jnp.zeros((8 - HEADS, ROWS), F32))
            out_ref[block, PART_ROWS:, :] = pack_lse(jnp.concatenate(lses, axis=0))


def times_transposed(values, weights):
    return lax.dot_general(
        values, weights, (((0,), (0,)), ((), ())), preferred_element_type=F32
    )


def in_vmem():
    return pl.BlockSpec(memory_space=pltpu.VMEM)


def anywhere():
    return pl.BlockSpec(memory_space=pl.ANY)


def in_smem():
    return pl.BlockSpec(memory_space=pltpu.SMEM)


def history(
    groups, counts, scale_index, scale_table, queries, keys, values, previous=None, after=()
):
    blocks = len(queries)
    operands = [*queries, keys, values]
    at = None
    if previous is not None:
        held, at = previous
        operands.append(held)
    return pl.pallas_call(
        functools.partial(history_kernel, blocks, at, len(after)),
        out_shape=jax.ShapeDtypeStruct((blocks, MSG_ROWS, ROWS), BF16),
        in_specs=[in_smem()] * 4 + [anywhere()] * len(after) + [in_vmem()] * len(operands),
        out_specs=in_vmem(),
        scratch_shapes=[pltpu.VMEM((HEADS, SLOTS, ROWS), BF16)],
        compiler_params=params(),
        cost_estimate=pl.CostEstimate(
            flops=4 * blocks * HEADS * ROWS * SLOTS * DH,
            bytes_accessed=2 * HEADS * SLOTS * DH * 2,
            transcendentals=blocks * HEADS * ROWS * SLOTS,
        ),
    )(groups, counts, scale_index, scale_table, *after, *operands)


def fresh_kernel(groups, q_ref, k_ref, v_ref, out_ref, lse_ref):
    column = lax.broadcasted_iota(I32, (ROWS, ROWS), 0)
    row = lax.broadcasted_iota(I32, (ROWS, ROWS), 1)
    visible = (column <= row) & ((column >= SPAN) | (row < SPAN))
    lses = []
    for head in range(HEADS):
        group = groups[head]
        raw = lax.dot_general(
            k_ref[group],
            q_ref[head * ROWS : (head + 1) * ROWS, :],
            (((1,), (1,)), ((), ())),
            preferred_element_type=F32,
        )
        score = jnp.where(visible, raw * (INVERSE * LOG2E), FLOOR)
        top = jnp.max(score, axis=0, keepdims=True)
        expo = jnp.exp2(score - top)
        total = jnp.sum(expo, axis=0, keepdims=True)
        mixed = times_transposed(v_ref[group], expo.astype(BF16))
        out_ref[head * DH : (head + 1) * DH, :] = mixed * (1.0 / total)
        lses.append(top + log2(total))
    lses.append(jnp.zeros((8 - HEADS, ROWS), F32))
    lse_ref[...] = jnp.concatenate(lses, axis=0)


def fresh_part(groups, query, new_keys, new_values):
    return pl.pallas_call(
        fresh_kernel,
        out_shape=(
            jax.ShapeDtypeStruct((PART_ROWS, ROWS), F32),
            jax.ShapeDtypeStruct((8, ROWS), F32),
        ),
        in_specs=[in_smem()] + [in_vmem()] * 3,
        out_specs=(in_vmem(), in_vmem()),
        compiler_params=params(),
        cost_estimate=pl.CostEstimate(
            flops=4 * HEADS * ROWS * ROWS * DH,
            bytes_accessed=HEADS * ROWS * DH * 6,
            transcendentals=HEADS * ROWS * ROWS,
        ),
    )(groups, query, new_keys, new_values)


def combine_kernel(a_ref, b_ref, c_ref, d_ref, fresh_ref, fresh_lse_ref, out_ref):
    parts = (a_ref, b_ref, c_ref, d_ref)
    lses = [unpack_lse(part[0, PART_ROWS:, :]) for part in parts]
    fresh_lse = fresh_lse_ref[...]
    peak = functools.reduce(jnp.maximum, lses, fresh_lse)
    weights = [jnp.exp2(lse - peak) for lse in lses]
    fresh_weight = jnp.exp2(fresh_lse - peak)
    inverse = 1.0 / functools.reduce(jnp.add, weights, fresh_weight)
    weights = [weight * inverse for weight in weights]
    fresh_weight = fresh_weight * inverse
    for head in range(HEADS):
        rows = slice(head * DH, (head + 1) * DH)
        total = fresh_ref[rows, :] * fresh_weight[head : head + 1]
        for part, weight in zip(parts, weights):
            total = total + part[0, rows, :].astype(F32) * weight[head : head + 1]
        out_ref[:, rows] = jnp.transpose(total).astype(BF16)


def combined(parts, fresh, fresh_lse):
    return pl.pallas_call(
        combine_kernel,
        out_shape=jax.ShapeDtypeStruct((ROWS, PART_ROWS), BF16),
        in_specs=[in_vmem()] * 6,
        out_specs=in_vmem(),
        compiler_params=params(),
        cost_estimate=pl.CostEstimate(
            flops=10 * ROWS * PART_ROWS, bytes_accessed=3 * 2**20, transcendentals=0
        ),
    )(*parts, fresh, fresh_lse)


def load_kernel(*refs):
    *refs, sems = refs
    sources, targets = refs[: len(refs) // 2], refs[len(refs) // 2 :]
    copies = []
    for source, target in zip(sources, targets):
        for group in range(target.shape[0]):
            copies.append(
                pltpu.make_async_copy(source.at[group], target.at[group], sems.at[len(copies)])
            )
    for copy in copies:
        copy.start()
    for copy in copies:
        copy.wait()


def loaded(*values):
    return pl.pallas_call(
        load_kernel,
        out_shape=[pltpu.VMEM(value.shape, BF16) for value in values],
        in_specs=[pl.BlockSpec(memory_space=pltpu.HBM)] * len(values),
        out_specs=[in_vmem()] * len(values),
        scratch_shapes=[pltpu.SemaphoreType.DMA((sum(value.shape[0] for value in values),))],
        compiler_params=params(),
        cost_estimate=pl.CostEstimate(
            flops=0,
            bytes_accessed=4 * sum(value.size for value in values),
            transcendentals=0,
        ),
    )(*[fixed(value, pltpu.HBM) for value in values])


def project_kernel(at, after_ref, w_ref, v_ref, a_ref, b_ref, out_ref, held_ref, sems):
    copies = []
    for block in range(out_ref.shape[0]):
        columns = pl.ds(pl.multiple_of(at[block] * ROWS, ROWS), ROWS)
        for side, ref in enumerate((w_ref, v_ref)):
            copies.append(
                pltpu.make_async_copy(
                    ref.at[:, columns], held_ref.at[block, side], sems.at[block, side]
                )
            )
    for copy in copies:
        copy.start()
    for block in range(out_ref.shape[0]):
        copies[2 * block].wait()
        copies[2 * block + 1].wait()
        total = jnp.dot(a_ref[...], held_ref[block, 0], preferred_element_type=F32)
        total = total + jnp.dot(b_ref[...], held_ref[block, 1], preferred_element_type=F32)
        out_ref[block] = total.astype(out_ref.dtype)


def projected(at, after, mine, theirs, weight, other_weight, kind):
    count = at.shape[0]
    depth = weight.shape[0]
    in_hbm = pl.BlockSpec(memory_space=pltpu.HBM)
    return pl.pallas_call(
        project_kernel,
        out_shape=jax.ShapeDtypeStruct((count, ROWS, ROWS), kind),
        in_specs=[in_smem(), anywhere(), in_hbm, in_hbm, in_vmem(), in_vmem()],
        out_specs=in_vmem(),
        scratch_shapes=[
            pltpu.VMEM((count, 2, depth, ROWS), BF16),
            pltpu.SemaphoreType.DMA((count, 2)),
        ],
        compiler_params=params(),
        cost_estimate=pl.CostEstimate(
            flops=count * 4 * ROWS * ROWS * depth,
            bytes_accessed=count * 4 * ROWS * depth,
            transcendentals=0,
        ),
    )(at, after, fixed(weight, pltpu.HBM), fixed(other_weight, pltpu.HBM), mine, theirs)


def advance_kernel(up_at, down_at, up_here, sums_ref, *refs):
    up_out, down_out = refs[-2:]
    arrived = list(refs[:-2])
    up, down = sums_ref[up_at], sums_ref[down_at]
    if up_here:
        up = up + arrived.pop(0)[0].astype(F32)
    if arrived:
        down = down + arrived.pop(0)[0].astype(F32)
    up_out[0] = up.astype(BF16)
    down_out[0] = down.astype(BF16)


def advanced(up_at, down_at, sums, up, down):
    kind = jax.ShapeDtypeStruct((1, ROWS, ROWS), BF16)
    operands = [sums] + [value for value in (up, down) if value is not None]
    return pl.pallas_call(
        functools.partial(advance_kernel, up_at, down_at, up is not None),
        out_shape=(kind, kind),
        in_specs=[in_vmem()] * len(operands),
        out_specs=(in_vmem(), in_vmem()),
        compiler_params=params(),
        cost_estimate=pl.CostEstimate(
            flops=2 * ROWS * ROWS, bytes_accessed=8 * ROWS * ROWS, transcendentals=0
        ),
    )(*operands)


def finish_kernel(at, sums_ref, up_ref, down_ref, out_ref):
    total = sums_ref[at] + (up_ref[0].astype(F32) + down_ref[0].astype(F32))
    out_ref[...] = total.astype(out_ref.dtype)


def finished(at, sums, up, down, kind):
    return pl.pallas_call(
        functools.partial(finish_kernel, at),
        out_shape=jax.ShapeDtypeStruct((ROWS, ROWS), kind),
        in_specs=[in_vmem()] * 3,
        out_specs=in_vmem(),
        compiler_params=params(),
        cost_estimate=pl.CostEstimate(
            flops=2 * ROWS * ROWS, bytes_accessed=8 * ROWS * ROWS, transcendentals=0
        ),
    )(sums, up, down)


def shards(
    queries,
    cache_keys,
    cache_values,
    scale_index,
    scale_table,
    hist_lengths,
    span_offsets,
    new_keys,
    new_values,
    head_groups,
    out_weight,
):
    ctx, place = lax.axis_index("ctx"), lax.axis_index("head")
    y, xh = ctx // 2, ctx % 2
    z, xl, core = place // 4, (place // 2) % 2, place % 2

    length = hist_lengths[0]
    facts = head_groups.astype(BF16)
    facts = jnp.pad(facts[None], ((0, FACT_ROWS - 1), (0, DH - facts.shape[0])))
    q0 = jnp.transpose(queries, (1, 0, 2)).reshape(HEADS * ROWS, DH)
    q0 = jnp.concatenate([q0, facts])
    p0 = send(q0, dxh=1, dxl=1)
    q_down = send(q0, dy=1)
    q_up = send(q0, dy=-1)
    q_far = send(q0, dy=2)
    p_down = send(p0, dy=1)
    p_up = send(p0, dy=-1)
    p_far = send(q_far, dxh=1, dxl=1)
    sent_weight = send(out_weight, dcore=1)
    keys, values = loaded(cache_keys, cache_values)
    fresh, fresh_lse = fresh_part(
        head_groups,
        q0,
        jnp.transpose(new_keys, (1, 0, 2)),
        jnp.transpose(new_values, (1, 0, 2)),
    )
    pair_groups = p0[HEADS * ROWS, :HEADS].astype(I32)
    lengths = lax.all_to_all(
        jnp.broadcast_to(hist_lengths, (8,)), "ctx", split_axis=0, concat_axis=0, tiled=True
    )
    start = jnp.sum(jnp.where(jnp.arange(8) < ctx, lengths, 0))

    def counts(source_y, source_xh):
        source = (source_y % 4) * 2 + source_xh
        offsets = lax.dynamic_slice_in_dim(span_offsets, source * 2, 2)
        return jnp.clip(jnp.minimum(length, offsets - start), 0, SLOTS)

    def attend(groups, sources, source_xh, queries, previous=None, after=()):
        return history(
            groups,
            jnp.concatenate([counts(y + step, source_xh) for step in sources]),
            scale_index,
            scale_table,
            queries,
            keys,
            values,
            previous,
            after,
        )

    first = attend(pair_groups, (0,), 1 - xh, [p0], None, (q_far,))
    back = {0: (send(first, dxh=1, dxl=1), 0)}
    for step, query in ((-1, p_down), (1, p_up), (2, p_far)):
        last = attend(pair_groups, (step,), 1 - xh, [query])
        back[step] = (send(last, dxh=1, dxl=1), 0)
    parts = []
    after = (last,)
    for step, query in ((0, q0), (-1, q_down), (1, q_up), (2, q_far)):
        part = attend(head_groups, (step,), xh, [query], back[step], after)
        after = (part,)
        parts.append(send(part, dy=step) if step else part)

    mine = combined(parts, fresh, fresh_lse)
    theirs = send(mine, dcore=1)

    def project(steps, kind, after):
        at = jnp.stack([(((z + step) % 8) * 2 + xl) ^ other for step, other in steps])
        return projected(2 * at + core, after, mine, theirs, out_weight, sent_weight, kind)

    first = project([(4, 0), (4, 1)], BF16, mine)
    up = send(first[0:1], dz=1)
    down = send(first[1:2], dz=-1)
    steps = ((3, 0), (3, 1), (-3, 0), (-3, 1))
    sums = project(steps, F32, first)
    theirs_up, theirs_down = advanced(1, 3, sums, None, down)
    mine_up, mine_down = advanced(0, 2, sums, up, None)
    steps = [(step, other) for step in (2, -2, 1, -1, 0) for other in (0, 1)]
    sums = project(steps, F32, theirs_up)
    for at in (0, 4, 8):
        theirs_up, theirs_down = send(theirs_up, dz=1), send(theirs_down, dz=-1)
        mine_up, mine_down = send(mine_up, dz=1), send(mine_down, dz=-1)
        if at < 8:
            theirs_up, theirs_down = advanced(at + 1, at + 3, sums, theirs_up, theirs_down)
            mine_up, mine_down = advanced(at, at + 2, sums, mine_up, mine_down)
    across = send(finished(9, sums, theirs_up, theirs_down, BF16), dxl=1)
    kept = finished(8, sums, mine_up, mine_down, F32)
    return (kept + across.astype(F32)).astype(BF16)


def solution(mesh):
    placed = (
        P("ctx", "head", None),
        P(None, "ctx", None),
        P(None, "ctx", None),
        P(None, "ctx"),
        P(),
        P("ctx"),
        P(),
        P("ctx", None, None),
        P("ctx", None, None),
        P("head"),
        P("head", None),
    )
    return jax.shard_map(
        shards, mesh=mesh, in_specs=placed, out_specs=P("ctx", "head"), check_vma=False
    )
```

```python
import functools
import math

import jax
import jax.numpy as jnp
from jax import lax
from jax.experimental import pallas as pl
from jax.experimental.pallas import tpu as pltpu
from jax.sharding import PartitionSpec as P

SPAN = 128
SBLK = 128
HEADS = 4
ROWS = 256
DH = 128
SLOTS = 768
BLOCKS = SLOTS // SBLK
PART_ROWS = HEADS * DH
LSE_ROWS = 16
FACT_ROWS = 16
MSG_ROWS = PART_ROWS + LSE_ROWS
FLOOR = -1e30
LOG2E = math.log2(math.e)
INVERSE = 1.0 / math.sqrt(DH)
AXES = ("ctx", "head")
F32, BF16, I32 = jnp.float32, jnp.bfloat16, jnp.int32
VMEM_LIMIT = 20 * 1024 * 1024


def linear(y, xh, z, xl, core):
    return (((y % 4) * 2 + xh % 2) * 8 + z % 8) * 4 + (xl % 2) * 2 + core % 2


def moved(dy=0, dxh=0, dz=0, dxl=0, dcore=0):
    return [
        (linear(y, xh, z, xl, c), linear(y + dy, xh + dxh, z + dz, xl + dxl, c + dcore))
        for y in range(4)
        for xh in range(2)
        for z in range(8)
        for xl in range(2)
        for c in range(2)
    ]


def send(value, **move):
    return lax.ppermute(value, AXES, moved(**move))


def params():
    return pltpu.CompilerParams(vmem_limit_bytes=VMEM_LIMIT)


def fixed(value, space=pltpu.VMEM):
    return pltpu.with_memory_space_constraint(value, space)


def log2(value):
    return jnp.log(value) * LOG2E


def pack_lse(lses):
    lse = jnp.concatenate(lses, axis=0)
    high = lse.astype(BF16).astype(F32)
    rest = lse - high
    middle = rest.astype(BF16).astype(F32)
    low = (rest - middle).astype(BF16).astype(F32)
    return jnp.concatenate([high, middle, low, jnp.zeros_like(low)], axis=0).astype(BF16)


def unpack_lse(packed):
    wide = packed.astype(F32)
    return wide[0:HEADS] + wide[HEADS : 2 * HEADS] + wide[2 * HEADS : 3 * HEADS]


def history_kernel(blocks, at, later, groups, counts, scale_index, scale_table, *refs):
    refs = refs[later:]
    q_refs, (k_ref, v_ref, *rest) = refs[:blocks], refs[blocks:]
    if at is not None:
        prev_ref, out_ref, weights_ref = rest
    else:
        out_ref, weights_ref = rest
    lane = lax.broadcasted_iota(I32, (1, ROWS), 1)
    slot = lax.broadcasted_iota(I32, (SBLK, ROWS), 0)
    units = [(block, head) for block in range(blocks) for head in range(HEADS)]

    def products(unit):
        block, head = units[unit]
        return lax.dot_general(
            k_ref[groups[head]],
            q_refs[block][head * ROWS : (head + 1) * ROWS, :],
            (((1,), (1,)), ((), ())),
            preferred_element_type=F32,
        )

    following = products(0)
    for unit, (block, head) in enumerate(units):
        if head == 0:
            lses = []
            count = jnp.where(lane < SPAN, counts[2 * block], counts[2 * block + 1])
            seen = count > 0
            if at is not None:
                held = unpack_lse(prev_ref[at, PART_ROWS:, :])
        group = groups[head]
        raw = following
        if unit + 1 < len(units):
            following = products(unit + 1)
        scores = []
        for part in range(BLOCKS):
            scale = scale_table[0, scale_index[group, part]] * (INVERSE * LOG2E)
            piece = raw[part * SBLK : (part + 1) * SBLK] * scale
            scores.append(jnp.where(slot < count - part * SBLK, piece, FLOOR))
        top = functools.reduce(jnp.maximum, scores)
        top = jnp.max(top, axis=0, keepdims=True)
        total = jnp.zeros((SBLK, ROWS), F32)
        for part in range(BLOCKS):
            scale = scale_table[1, scale_index[group, part]]
            expo = jnp.exp2(scores[part] - top)
            total = total + expo
            weights_ref[head, part * SBLK : (part + 1) * SBLK, :] = (expo * scale).astype(BF16)
        total = jnp.sum(total, axis=0, keepdims=True)
        mixed = times_transposed(v_ref[group], weights_ref[head])
        lse = jnp.where(seen, top + log2(total), FLOOR)
        share = jnp.where(seen, 1.0 / total, 0.0)
        rows = slice(head * DH, (head + 1) * DH)
        if at is not None:
            before = held[head : head + 1]
            peak = jnp.maximum(lse, before)
            mine = jnp.exp2(lse - peak)
            other = jnp.exp2(before - peak)
            both = mine + other
            inverse = 1.0 / both
            mixed = mixed * (share * mine * inverse)
            mixed = mixed + prev_ref[at, rows, :].astype(F32) * (other * inverse)
            lse = peak + log2(both)
        else:
            mixed = mixed * share
        out_ref[block, rows, :] = mixed.astype(BF16)
        lses.append(lse)
        if head == HEADS - 1:
            out_ref[block, PART_ROWS:, :] = pack_lse(lses)


def times_transposed(values, weights):
    return lax.dot_general(
        values, weights, (((0,), (0,)), ((), ())), preferred_element_type=F32
    )


def in_vmem():
    return pl.BlockSpec(memory_space=pltpu.VMEM)


def anywhere():
    return pl.BlockSpec(memory_space=pl.ANY)


def in_smem():
    return pl.BlockSpec(memory_space=pltpu.SMEM)


def history(
    groups, counts, scale_index, scale_table, queries, keys, values, previous=None, after=()
):
    blocks = len(queries)
    operands = [*queries, keys, values]
    at = None
    if previous is not None:
        held, at = previous
        operands.append(held)
    return pl.pallas_call(
        functools.partial(history_kernel, blocks, at, len(after)),
        out_shape=jax.ShapeDtypeStruct((blocks, MSG_ROWS, ROWS), BF16),
        in_specs=[in_smem()] * 4 + [anywhere()] * len(after) + [in_vmem()] * len(operands),
        out_specs=in_vmem(),
        scratch_shapes=[pltpu.VMEM((HEADS, SLOTS, ROWS), BF16)],
        compiler_params=params(),
        cost_estimate=pl.CostEstimate(
            flops=4 * blocks * HEADS * ROWS * SLOTS * DH,
            bytes_accessed=2 * HEADS * SLOTS * DH * 2,
            transcendentals=blocks * HEADS * ROWS * SLOTS,
        ),
    )(groups, counts, scale_index, scale_table, *after, *operands)


def fresh_kernel(groups, q_ref, k_ref, v_ref, out_ref, lse_ref):
    column = lax.broadcasted_iota(I32, (ROWS, ROWS), 0)
    row = lax.broadcasted_iota(I32, (ROWS, ROWS), 1)
    visible = (column <= row) & ((column >= SPAN) | (row < SPAN))
    lses = []
    for head in range(HEADS):
        group = groups[head]
        raw = lax.dot_general(
            k_ref[group],
            q_ref[head * ROWS : (head + 1) * ROWS, :],
            (((1,), (1,)), ((), ())),
            preferred_element_type=F32,
        )
        score = jnp.where(visible, raw * (INVERSE * LOG2E), FLOOR)
        top = jnp.max(score, axis=0, keepdims=True)
        expo = jnp.exp2(score - top)
        total = jnp.sum(expo, axis=0, keepdims=True)
        mixed = times_transposed(v_ref[group], expo.astype(BF16))
        out_ref[head * DH : (head + 1) * DH, :] = mixed * (1.0 / total)
        lses.append(top + log2(total))
    lses.append(jnp.zeros((8 - HEADS, ROWS), F32))
    lse_ref[...] = jnp.concatenate(lses, axis=0)


def fresh_part(groups, query, new_keys, new_values):
    return pl.pallas_call(
        fresh_kernel,
        out_shape=(
            jax.ShapeDtypeStruct((PART_ROWS, ROWS), F32),
            jax.ShapeDtypeStruct((8, ROWS), F32),
        ),
        in_specs=[in_smem()] + [in_vmem()] * 3,
        out_specs=(in_vmem(), in_vmem()),
        compiler_params=params(),
        cost_estimate=pl.CostEstimate(
            flops=4 * HEADS * ROWS * ROWS * DH,
            bytes_accessed=HEADS * ROWS * DH * 6,
            transcendentals=HEADS * ROWS * ROWS,
        ),
    )(groups, query, new_keys, new_values)


def combine_kernel(a_ref, b_ref, c_ref, d_ref, fresh_ref, fresh_lse_ref, out_ref):
    parts = (a_ref, b_ref, c_ref, d_ref)
    lses = [unpack_lse(part[0, PART_ROWS:, :]) for part in parts]
    fresh_lse = fresh_lse_ref[0:HEADS, :]
    peak = functools.reduce(jnp.maximum, lses, fresh_lse)
    weights = [jnp.exp2(lse - peak) for lse in lses]
    fresh_weight = jnp.exp2(fresh_lse - peak)
    inverse = 1.0 / functools.reduce(jnp.add, weights, fresh_weight)
    weights = [weight * inverse for weight in weights]
    fresh_weight = fresh_weight * inverse
    for head in range(HEADS):
        rows = slice(head * DH, (head + 1) * DH)
        total = fresh_ref[rows, :] * fresh_weight[head : head + 1]
        for part, weight in zip(parts, weights):
            total = total + part[0, rows, :].astype(F32) * weight[head : head + 1]
        out_ref[:, rows] = jnp.transpose(total).astype(BF16)


def combined(parts, fresh, fresh_lse):
    return pl.pallas_call(
        combine_kernel,
        out_shape=jax.ShapeDtypeStruct((ROWS, PART_ROWS), BF16),
        in_specs=[in_vmem()] * 6,
        out_specs=in_vmem(),
        compiler_params=params(),
        cost_estimate=pl.CostEstimate(
            flops=10 * ROWS * PART_ROWS, bytes_accessed=3 * 2**20, transcendentals=0
        ),
    )(*parts, fresh, fresh_lse)


def load_kernel(*refs):
    *refs, sems = refs
    sources, targets = refs[: len(refs) // 2], refs[len(refs) // 2 :]
    copies = []
    for source, target in zip(sources, targets):
        for group in range(target.shape[0]):
            copies.append(
                pltpu.make_async_copy(source.at[group], target.at[group], sems.at[len(copies)])
            )
    for copy in copies:
        copy.start()
    for copy in copies:
        copy.wait()


def loaded(*values):
    return pl.pallas_call(
        load_kernel,
        out_shape=[pltpu.VMEM(value.shape, BF16) for value in values],
        in_specs=[pl.BlockSpec(memory_space=pltpu.HBM)] * len(values),
        out_specs=[in_vmem()] * len(values),
        scratch_shapes=[pltpu.SemaphoreType.DMA((sum(value.shape[0] for value in values),))],
        compiler_params=params(),
        cost_estimate=pl.CostEstimate(
            flops=0,
            bytes_accessed=4 * sum(value.size for value in values),
            transcendentals=0,
        ),
    )(*[fixed(value, pltpu.HBM) for value in values])


def project_kernel(at, after_ref, w_ref, v_ref, a_ref, b_ref, out_ref, held_ref, sems):
    copies = []
    for block in range(out_ref.shape[0]):
        columns = pl.ds(pl.multiple_of(at[block] * ROWS, ROWS), ROWS)
        for side, ref in enumerate((w_ref, v_ref)):
            copies.append(
                pltpu.make_async_copy(
                    ref.at[:, columns], held_ref.at[block, side], sems.at[block, side]
                )
            )
    for copy in copies:
        copy.start()
    for block in range(out_ref.shape[0]):
        copies[2 * block].wait()
        copies[2 * block + 1].wait()
        total = jnp.dot(a_ref[...], held_ref[block, 0], preferred_element_type=F32)
        total = total + jnp.dot(b_ref[...], held_ref[block, 1], preferred_element_type=F32)
        out_ref[block] = total.astype(out_ref.dtype)


def project_mine_kernel(at, w_ref, v_ref, a_ref, out_ref, other_ref, held_ref, sems):
    copies = []
    for block in range(out_ref.shape[0]):
        columns = pl.ds(pl.multiple_of(at[block] * ROWS, ROWS), ROWS)
        for side, (source, target) in enumerate(((w_ref, held_ref), (v_ref, other_ref))):
            copies.append(
                pltpu.make_async_copy(
                    source.at[:, columns], target.at[block], sems.at[block, side]
                )
            )
    for copy in copies:
        copy.start()
    for block in range(out_ref.shape[0]):
        copies[2 * block].wait()
        out_ref[block] = jnp.dot(a_ref[...], held_ref[block], preferred_element_type=F32)
    for block in range(out_ref.shape[0]):
        copies[2 * block + 1].wait()


def project_theirs_kernel(before_ref, v_ref, b_ref, out_ref):
    for block in range(out_ref.shape[0]):
        total = jnp.dot(b_ref[...], v_ref[block], preferred_element_type=F32)
        out_ref[block] = (before_ref[block] + total).astype(BF16)


def projected_mine(at, mine, weight, other_weight):
    count = at.shape[0]
    depth = weight.shape[0]
    in_hbm = pl.BlockSpec(memory_space=pltpu.HBM)
    return pl.pallas_call(
        project_mine_kernel,
        out_shape=(
            jax.ShapeDtypeStruct((count, ROWS, ROWS), F32),
            jax.ShapeDtypeStruct((count, depth, ROWS), BF16),
        ),
        in_specs=[in_smem(), in_hbm, in_hbm, in_vmem()],
        out_specs=(in_vmem(), in_vmem()),
        scratch_shapes=[
            pltpu.VMEM((count, depth, ROWS), BF16),
            pltpu.SemaphoreType.DMA((count, 2)),
        ],
        compiler_params=params(),
        cost_estimate=pl.CostEstimate(
            flops=count * 2 * ROWS * ROWS * depth,
            bytes_accessed=count * 4 * ROWS * depth,
            transcendentals=0,
        ),
    )(at, fixed(weight, pltpu.HBM), fixed(other_weight, pltpu.HBM), mine)


def projected_theirs(before, other_weight, theirs):
    return pl.pallas_call(
        project_theirs_kernel,
        out_shape=jax.ShapeDtypeStruct(before.shape, BF16),
        in_specs=[in_vmem()] * 3,
        out_specs=in_vmem(),
        compiler_params=params(),
        cost_estimate=pl.CostEstimate(
            flops=2 * before.size * other_weight.shape[1],
            bytes_accessed=before.size * 8,
            transcendentals=0,
        ),
    )(before, other_weight, theirs)


def projected(at, after, mine, theirs, weight, other_weight, kind):
    count = at.shape[0]
    depth = weight.shape[0]
    in_hbm = pl.BlockSpec(memory_space=pltpu.HBM)
    return pl.pallas_call(
        project_kernel,
        out_shape=jax.ShapeDtypeStruct((count, ROWS, ROWS), kind),
        in_specs=[in_smem(), anywhere(), in_hbm, in_hbm, in_vmem(), in_vmem()],
        out_specs=in_vmem(),
        scratch_shapes=[
            pltpu.VMEM((count, 2, depth, ROWS), BF16),
            pltpu.SemaphoreType.DMA((count, 2)),
        ],
        compiler_params=params(),
        cost_estimate=pl.CostEstimate(
            flops=count * 4 * ROWS * ROWS * depth,
            bytes_accessed=count * 4 * ROWS * depth,
            transcendentals=0,
        ),
    )(at, after, fixed(weight, pltpu.HBM), fixed(other_weight, pltpu.HBM), mine, theirs)


def advance_kernel(up_at, down_at, up_here, sums_ref, *refs):
    up_out, down_out = refs[-2:]
    arrived = list(refs[:-2])
    up, down = sums_ref[up_at], sums_ref[down_at]
    if up_here:
        up = up + arrived.pop(0)[0].astype(F32)
    if arrived:
        down = down + arrived.pop(0)[0].astype(F32)
    up_out[0] = up.astype(BF16)
    down_out[0] = down.astype(BF16)


def advanced(up_at, down_at, sums, up, down):
    kind = jax.ShapeDtypeStruct((1, ROWS, ROWS), BF16)
    operands = [sums] + [value for value in (up, down) if value is not None]
    return pl.pallas_call(
        functools.partial(advance_kernel, up_at, down_at, up is not None),
        out_shape=(kind, kind),
        in_specs=[in_vmem()] * len(operands),
        out_specs=(in_vmem(), in_vmem()),
        compiler_params=params(),
        cost_estimate=pl.CostEstimate(
            flops=2 * ROWS * ROWS, bytes_accessed=8 * ROWS * ROWS, transcendentals=0
        ),
    )(*operands)


def finish_kernel(at, sums_ref, up_ref, down_ref, out_ref):
    total = sums_ref[at] + (up_ref[0].astype(F32) + down_ref[0].astype(F32))
    out_ref[...] = total.astype(out_ref.dtype)


def finished(at, sums, up, down, kind):
    return pl.pallas_call(
        functools.partial(finish_kernel, at),
        out_shape=jax.ShapeDtypeStruct((ROWS, ROWS), kind),
        in_specs=[in_vmem()] * 3,
        out_specs=in_vmem(),
        compiler_params=params(),
        cost_estimate=pl.CostEstimate(
            flops=2 * ROWS * ROWS, bytes_accessed=8 * ROWS * ROWS, transcendentals=0
        ),
    )(sums, up, down)


def shards(
    queries,
    cache_keys,
    cache_values,
    scale_index,
    scale_table,
    hist_lengths,
    span_offsets,
    new_keys,
    new_values,
    head_groups,
    out_weight,
):
    ctx, place = lax.axis_index("ctx"), lax.axis_index("head")
    y, xh = ctx // 2, ctx % 2
    z, xl, core = place // 4, (place // 2) % 2, place % 2

    length = hist_lengths[0]
    facts = head_groups.astype(BF16)
    facts = jnp.pad(facts[None], ((0, FACT_ROWS - 1), (0, DH - facts.shape[0])))
    q0 = jnp.transpose(queries, (1, 0, 2)).reshape(HEADS * ROWS, DH)
    q0 = jnp.concatenate([q0, facts])
    p0 = send(q0, dxh=1, dxl=1)
    q_down = send(q0, dy=1)
    q_up = send(q0, dy=-1)
    p_down = send(p0, dy=1)
    p_up = send(p0, dy=-1)
    q_far = send(q_up, dy=-1)
    sent_weight = send(out_weight, dcore=1)
    keys, values = loaded(cache_keys, cache_values)
    fresh, fresh_lse = fresh_part(
        head_groups,
        q0,
        jnp.transpose(new_keys, (1, 0, 2)),
        jnp.transpose(new_values, (1, 0, 2)),
    )
    pair_groups = p0[HEADS * ROWS, :HEADS].astype(I32)
    lengths = lax.all_to_all(
        jnp.broadcast_to(hist_lengths, (8,)), "ctx", split_axis=0, concat_axis=0, tiled=True
    )
    start = jnp.sum(jnp.where(jnp.arange(8) < ctx, lengths, 0))

    def counts(source_y, source_xh):
        source = (source_y % 4) * 2 + source_xh
        offsets = lax.dynamic_slice_in_dim(span_offsets, source * 2, 2)
        return jnp.clip(jnp.minimum(length, offsets - start), 0, SLOTS)

    def attend(groups, sources, source_xh, queries, previous=None, after=()):
        return history(
            groups,
            jnp.concatenate([counts(y + step, source_xh) for step in sources]),
            scale_index,
            scale_table,
            queries,
            keys,
            values,
            previous,
            after,
        )

    first = attend(pair_groups, (0,), 1 - xh, [p0])
    back = {0: (send(first, dxh=1, dxl=1), 0)}
    p_down, _ = lax.optimization_barrier((p_down, first))
    p_far = send(p_down, dy=1)
    for step, query in ((-1, p_down), (1, p_up), (2, p_far)):
        last = attend(pair_groups, (step,), 1 - xh, [query])
        back[step] = (send(last, dxh=1, dxl=1), 0)
    parts = []
    after = (last,)
    for step, query in ((0, q0), (-1, q_down), (1, q_up), (2, q_far)):
        part = attend(head_groups, (step,), xh, [query], back[step], after)
        after = (part,)
        parts.append(send(part, dy=step) if step else part)

    mine = combined(parts, fresh, fresh_lse)
    theirs = send(mine, dcore=1)

    def columns(steps):
        blocks = [(((z + step) % 8) * 2 + xl) ^ other for step, other in steps]
        return 2 * jnp.stack(blocks) + core

    def project(steps, kind, after):
        at = columns(steps)
        return projected(at, after, mine, theirs, out_weight, sent_weight, kind)

    at = columns([(4, 0), (4, 1)])
    first, fetched = projected_mine(at, mine, out_weight, sent_weight)
    first = projected_theirs(first, fetched, theirs)
    up = send(first[0:1], dz=1)
    down = send(first[1:2], dz=-1)
    steps = ((3, 0), (3, 1), (-3, 0), (-3, 1))
    sums = project(steps, F32, first)
    theirs_up, theirs_down = advanced(1, 3, sums, None, down)
    mine_up, mine_down = advanced(0, 2, sums, up, None)
    for step in (2, 1, 0):
        steps = ((step, 0), (step, 1), (-step, 0), (-step, 1))
        sums = project(steps if step else steps[:2], F32, theirs_up)
        theirs_up, theirs_down = send(theirs_up, dz=1), send(theirs_down, dz=-1)
        mine_up, mine_down = send(mine_up, dz=1), send(mine_down, dz=-1)
        if step:
            theirs_up, theirs_down = advanced(1, 3, sums, theirs_up, theirs_down)
            mine_up, mine_down = advanced(0, 2, sums, mine_up, mine_down)
    across = send(finished(1, sums, theirs_up, theirs_down, BF16), dxl=1)
    kept = finished(0, sums, mine_up, mine_down, F32)
    return (kept + across.astype(F32)).astype(BF16)


def solution(mesh):
    placed = (
        P("ctx", "head", None),
        P(None, "ctx", None),
        P(None, "ctx", None),
        P(None, "ctx"),
        P(),
        P("ctx"),
        P(),
        P("ctx", None, None),
        P("ctx", None, None),
        P("head"),
        P("head", None),
    )
    return jax.shard_map(
        shards, mesh=mesh, in_specs=placed, out_specs=P("ctx", "head"), check_vma=False
    )
```

```python
import functools
import math

import jax
import jax.numpy as jnp
from jax import lax
from jax.experimental import pallas as pl
from jax.experimental.pallas import tpu as pltpu
from jax.sharding import PartitionSpec as P

SPAN = 128
SBLK = 128
HEADS = 4
ROWS = 256
DH = 128
SLOTS = 768
BLOCKS = SLOTS // SBLK
PART_ROWS = HEADS * DH
LSE_ROWS = 16
FACT_ROWS = 16
MSG_ROWS = PART_ROWS + LSE_ROWS
FLOOR = -1e30
LOG2E = math.log2(math.e)
INVERSE = 1.0 / math.sqrt(DH)
AXES = ("ctx", "head")
F32, BF16, I32 = jnp.float32, jnp.bfloat16, jnp.int32
VMEM_LIMIT = 20 * 1024 * 1024


def linear(y, xh, z, xl, core):
    return (((y % 4) * 2 + xh % 2) * 8 + z % 8) * 4 + (xl % 2) * 2 + core % 2


def moved(dy=0, dxh=0, dz=0, dxl=0, dcore=0):
    return [
        (linear(y, xh, z, xl, c), linear(y + dy, xh + dxh, z + dz, xl + dxl, c + dcore))
        for y in range(4)
        for xh in range(2)
        for z in range(8)
        for xl in range(2)
        for c in range(2)
    ]


def send(value, **move):
    return lax.ppermute(value, AXES, moved(**move))


def params():
    return pltpu.CompilerParams(vmem_limit_bytes=VMEM_LIMIT)


def fixed(value, space=pltpu.VMEM):
    return pltpu.with_memory_space_constraint(value, space)


def log2(value):
    return jnp.log(value) * LOG2E


def pack_lse(lses):
    lse = jnp.concatenate(lses, axis=0)
    high = lse.astype(BF16).astype(F32)
    rest = lse - high
    middle = rest.astype(BF16).astype(F32)
    low = (rest - middle).astype(BF16).astype(F32)
    return jnp.concatenate([high, middle, low, jnp.zeros_like(low)], axis=0).astype(BF16)


def unpack_lse(packed):
    wide = packed.astype(F32)
    return wide[0:HEADS] + wide[HEADS : 2 * HEADS] + wide[2 * HEADS : 3 * HEADS]


def history_kernel(blocks, at, later, groups, counts, scale_index, scale_table, *refs):
    refs = refs[later:]
    q_refs, (k_ref, v_ref, *rest) = refs[:blocks], refs[blocks:]
    if at is not None:
        prev_ref, out_ref, weights_ref = rest
    else:
        out_ref, weights_ref = rest
    lane = lax.broadcasted_iota(I32, (1, ROWS), 1)
    slot = lax.broadcasted_iota(I32, (SBLK, ROWS), 0)
    units = [(block, head) for block in range(blocks) for head in range(HEADS)]

    def products(unit):
        block, head = units[unit]
        return lax.dot_general(
            k_ref[groups[head]],
            q_refs[block][head * ROWS : (head + 1) * ROWS, :],
            (((1,), (1,)), ((), ())),
            preferred_element_type=F32,
        )

    following = products(0)
    for unit, (block, head) in enumerate(units):
        if head == 0:
            lses = []
            count = jnp.where(lane < SPAN, counts[2 * block], counts[2 * block + 1])
            seen = count > 0
            if at is not None:
                held = unpack_lse(prev_ref[at, PART_ROWS:, :])
        group = groups[head]
        raw = following
        if unit + 1 < len(units):
            following = products(unit + 1)
        scores = []
        for part in range(BLOCKS):
            scale = scale_table[0, scale_index[group, part]] * (INVERSE * LOG2E)
            piece = raw[part * SBLK : (part + 1) * SBLK] * scale
            scores.append(jnp.where(slot < count - part * SBLK, piece, FLOOR))
        top = functools.reduce(jnp.maximum, scores)
        top = jnp.max(top, axis=0, keepdims=True)
        total = jnp.zeros((SBLK, ROWS), F32)
        for part in range(BLOCKS):
            scale = scale_table[1, scale_index[group, part]]
            expo = jnp.exp2(scores[part] - top)
            total = total + expo
            weights_ref[head, part * SBLK : (part + 1) * SBLK, :] = (expo * scale).astype(BF16)
        total = jnp.sum(total, axis=0, keepdims=True)
        mixed = times_transposed(v_ref[group], weights_ref[head])
        lse = jnp.where(seen, top + log2(total), FLOOR)
        share = jnp.where(seen, 1.0 / total, 0.0)
        rows = slice(head * DH, (head + 1) * DH)
        if at is not None:
            before = held[head : head + 1]
            peak = jnp.maximum(lse, before)
            mine = jnp.exp2(lse - peak)
            other = jnp.exp2(before - peak)
            both = mine + other
            inverse = 1.0 / both
            mixed = mixed * (share * mine * inverse)
            mixed = mixed + prev_ref[at, rows, :].astype(F32) * (other * inverse)
            lse = peak + log2(both)
        else:
            mixed = mixed * share
        out_ref[block, rows, :] = mixed.astype(BF16)
        lses.append(lse)
        if head == HEADS - 1:
            out_ref[block, PART_ROWS:, :] = pack_lse(lses)


def times_transposed(values, weights):
    return lax.dot_general(
        values, weights, (((0,), (0,)), ((), ())), preferred_element_type=F32
    )


def in_vmem():
    return pl.BlockSpec(memory_space=pltpu.VMEM)


def anywhere():
    return pl.BlockSpec(memory_space=pl.ANY)


def in_smem():
    return pl.BlockSpec(memory_space=pltpu.SMEM)


def history(
    groups, counts, scale_index, scale_table, queries, keys, values, previous=None, after=()
):
    blocks = len(queries)
    operands = [*queries, keys, values]
    at = None
    if previous is not None:
        held, at = previous
        operands.append(held)
    return pl.pallas_call(
        functools.partial(history_kernel, blocks, at, len(after)),
        out_shape=jax.ShapeDtypeStruct((blocks, MSG_ROWS, ROWS), BF16),
        in_specs=[in_smem()] * 4 + [anywhere()] * len(after) + [in_vmem()] * len(operands),
        out_specs=in_vmem(),
        scratch_shapes=[pltpu.VMEM((HEADS, SLOTS, ROWS), BF16)],
        compiler_params=params(),
        cost_estimate=pl.CostEstimate(
            flops=4 * blocks * HEADS * ROWS * SLOTS * DH,
            bytes_accessed=2 * HEADS * SLOTS * DH * 2,
            transcendentals=blocks * HEADS * ROWS * SLOTS,
        ),
    )(groups, counts, scale_index, scale_table, *after, *operands)


def fresh_kernel(groups, q_ref, k_ref, v_ref, out_ref, lse_ref):
    column = lax.broadcasted_iota(I32, (ROWS, ROWS), 0)
    row = lax.broadcasted_iota(I32, (ROWS, ROWS), 1)
    visible = (column <= row) & ((column >= SPAN) | (row < SPAN))
    lses = []
    for head in range(HEADS):
        group = groups[head]
        raw = lax.dot_general(
            k_ref[group],
            q_ref[head * ROWS : (head + 1) * ROWS, :],
            (((1,), (1,)), ((), ())),
            preferred_element_type=F32,
        )
        score = jnp.where(visible, raw * (INVERSE * LOG2E), FLOOR)
        top = jnp.max(score, axis=0, keepdims=True)
        expo = jnp.exp2(score - top)
        total = jnp.sum(expo, axis=0, keepdims=True)
        mixed = times_transposed(v_ref[group], expo.astype(BF16))
        out_ref[head * DH : (head + 1) * DH, :] = mixed * (1.0 / total)
        lses.append(top + log2(total))
    lses.append(jnp.zeros((8 - HEADS, ROWS), F32))
    lse_ref[...] = jnp.concatenate(lses, axis=0)


def fresh_part(groups, query, new_keys, new_values):
    return pl.pallas_call(
        fresh_kernel,
        out_shape=(
            jax.ShapeDtypeStruct((PART_ROWS, ROWS), F32),
            jax.ShapeDtypeStruct((8, ROWS), F32),
        ),
        in_specs=[in_smem()] + [in_vmem()] * 3,
        out_specs=(in_vmem(), in_vmem()),
        compiler_params=params(),
        cost_estimate=pl.CostEstimate(
            flops=4 * HEADS * ROWS * ROWS * DH,
            bytes_accessed=HEADS * ROWS * DH * 6,
            transcendentals=HEADS * ROWS * ROWS,
        ),
    )(groups, query, new_keys, new_values)


def combine_kernel(a_ref, b_ref, c_ref, d_ref, fresh_ref, fresh_lse_ref, out_ref):
    parts = (a_ref, b_ref, c_ref, d_ref)
    lses = [unpack_lse(part[0, PART_ROWS:, :]) for part in parts]
    fresh_lse = fresh_lse_ref[0:HEADS, :]
    peak = functools.reduce(jnp.maximum, lses, fresh_lse)
    weights = [jnp.exp2(lse - peak) for lse in lses]
    fresh_weight = jnp.exp2(fresh_lse - peak)
    inverse = 1.0 / functools.reduce(jnp.add, weights, fresh_weight)
    weights = [weight * inverse for weight in weights]
    fresh_weight = fresh_weight * inverse
    for head in range(HEADS):
        rows = slice(head * DH, (head + 1) * DH)
        total = fresh_ref[rows, :] * fresh_weight[head : head + 1]
        for part, weight in zip(parts, weights):
            total = total + part[0, rows, :].astype(F32) * weight[head : head + 1]
        out_ref[:, rows] = jnp.transpose(total).astype(BF16)


def combined(parts, fresh, fresh_lse):
    return pl.pallas_call(
        combine_kernel,
        out_shape=jax.ShapeDtypeStruct((ROWS, PART_ROWS), BF16),
        in_specs=[in_vmem()] * 6,
        out_specs=in_vmem(),
        compiler_params=params(),
        cost_estimate=pl.CostEstimate(
            flops=10 * ROWS * PART_ROWS, bytes_accessed=3 * 2**20, transcendentals=0
        ),
    )(*parts, fresh, fresh_lse)


def load_kernel(*refs):
    *refs, sems = refs
    sources, targets = refs[: len(refs) // 2], refs[len(refs) // 2 :]
    copies = []
    for source, target in zip(sources, targets):
        for group in range(target.shape[0]):
            copies.append(
                pltpu.make_async_copy(source.at[group], target.at[group], sems.at[len(copies)])
            )
    for copy in copies:
        copy.start()
    for copy in copies:
        copy.wait()


def loaded(*values):
    return pl.pallas_call(
        load_kernel,
        out_shape=[pltpu.VMEM(value.shape, BF16) for value in values],
        in_specs=[pl.BlockSpec(memory_space=pltpu.HBM)] * len(values),
        out_specs=[in_vmem()] * len(values),
        scratch_shapes=[pltpu.SemaphoreType.DMA((sum(value.shape[0] for value in values),))],
        compiler_params=params(),
        cost_estimate=pl.CostEstimate(
            flops=0,
            bytes_accessed=4 * sum(value.size for value in values),
            transcendentals=0,
        ),
    )(*[fixed(value, pltpu.HBM) for value in values])


def project_kernel(at, after_ref, w_ref, v_ref, a_ref, b_ref, out_ref, held_ref, sems):
    copies = []
    for block in range(out_ref.shape[0]):
        columns = pl.ds(pl.multiple_of(at[block] * ROWS, ROWS), ROWS)
        for side, ref in enumerate((w_ref, v_ref)):
            copies.append(
                pltpu.make_async_copy(
                    ref.at[:, columns], held_ref.at[block, side], sems.at[block, side]
                )
            )
    for copy in copies:
        copy.start()
    for block in range(out_ref.shape[0]):
        copies[2 * block].wait()
        copies[2 * block + 1].wait()
        total = jnp.dot(a_ref[...], held_ref[block, 0], preferred_element_type=F32)
        total = total + jnp.dot(b_ref[...], held_ref[block, 1], preferred_element_type=F32)
        out_ref[block] = total.astype(out_ref.dtype)


def project_mine_kernel(at, w_ref, v_ref, a_ref, out_ref, other_ref, held_ref, sems):
    copies = []
    for block in range(out_ref.shape[0]):
        columns = pl.ds(pl.multiple_of(at[block] * ROWS, ROWS), ROWS)
        for side, (source, target) in enumerate(((w_ref, held_ref), (v_ref, other_ref))):
            copies.append(
                pltpu.make_async_copy(
                    source.at[:, columns], target.at[block], sems.at[block, side]
                )
            )
    for copy in copies:
        copy.start()
    for block in range(out_ref.shape[0]):
        copies[2 * block].wait()
        out_ref[block] = jnp.dot(a_ref[...], held_ref[block], preferred_element_type=F32)
    for block in range(out_ref.shape[0]):
        copies[2 * block + 1].wait()


def project_theirs_kernel(before_ref, v_ref, b_ref, out_ref):
    for block in range(out_ref.shape[0]):
        total = jnp.dot(b_ref[...], v_ref[block], preferred_element_type=F32)
        out_ref[block] = (before_ref[block] + total).astype(BF16)


def projected_mine(at, mine, weight, other_weight):
    count = at.shape[0]
    depth = weight.shape[0]
    in_hbm = pl.BlockSpec(memory_space=pltpu.HBM)
    return pl.pallas_call(
        project_mine_kernel,
        out_shape=(
            jax.ShapeDtypeStruct((count, ROWS, ROWS), F32),
            jax.ShapeDtypeStruct((count, depth, ROWS), BF16),
        ),
        in_specs=[in_smem(), in_hbm, in_hbm, in_vmem()],
        out_specs=(in_vmem(), in_vmem()),
        scratch_shapes=[
            pltpu.VMEM((count, depth, ROWS), BF16),
            pltpu.SemaphoreType.DMA((count, 2)),
        ],
        compiler_params=params(),
        cost_estimate=pl.CostEstimate(
            flops=count * 2 * ROWS * ROWS * depth,
            bytes_accessed=count * 4 * ROWS * depth,
            transcendentals=0,
        ),
    )(at, fixed(weight, pltpu.HBM), fixed(other_weight, pltpu.HBM), mine)


def projected_theirs(before, other_weight, theirs):
    return pl.pallas_call(
        project_theirs_kernel,
        out_shape=jax.ShapeDtypeStruct(before.shape, BF16),
        in_specs=[in_vmem()] * 3,
        out_specs=in_vmem(),
        compiler_params=params(),
        cost_estimate=pl.CostEstimate(
            flops=2 * before.size * other_weight.shape[1],
            bytes_accessed=before.size * 8,
            transcendentals=0,
        ),
    )(before, other_weight, theirs)


def projected(at, after, mine, theirs, weight, other_weight, kind):
    count = at.shape[0]
    depth = weight.shape[0]
    in_hbm = pl.BlockSpec(memory_space=pltpu.HBM)
    return pl.pallas_call(
        project_kernel,
        out_shape=jax.ShapeDtypeStruct((count, ROWS, ROWS), kind),
        in_specs=[in_smem(), anywhere(), in_hbm, in_hbm, in_vmem(), in_vmem()],
        out_specs=in_vmem(),
        scratch_shapes=[
            pltpu.VMEM((count, 2, depth, ROWS), BF16),
            pltpu.SemaphoreType.DMA((count, 2)),
        ],
        compiler_params=params(),
        cost_estimate=pl.CostEstimate(
            flops=count * 4 * ROWS * ROWS * depth,
            bytes_accessed=count * 4 * ROWS * depth,
            transcendentals=0,
        ),
    )(at, after, fixed(weight, pltpu.HBM), fixed(other_weight, pltpu.HBM), mine, theirs)


def advance_kernel(up_at, down_at, up_here, sums_ref, *refs):
    up_out, down_out = refs[-2:]
    arrived = list(refs[:-2])
    up, down = sums_ref[up_at], sums_ref[down_at]
    if up_here:
        up = up + arrived.pop(0)[0].astype(F32)
    if arrived:
        down = down + arrived.pop(0)[0].astype(F32)
    up_out[0] = up.astype(BF16)
    down_out[0] = down.astype(BF16)


def advanced(up_at, down_at, sums, up, down):
    kind = jax.ShapeDtypeStruct((1, ROWS, ROWS), BF16)
    operands = [sums] + [value for value in (up, down) if value is not None]
    return pl.pallas_call(
        functools.partial(advance_kernel, up_at, down_at, up is not None),
        out_shape=(kind, kind),
        in_specs=[in_vmem()] * len(operands),
        out_specs=(in_vmem(), in_vmem()),
        compiler_params=params(),
        cost_estimate=pl.CostEstimate(
            flops=2 * ROWS * ROWS, bytes_accessed=8 * ROWS * ROWS, transcendentals=0
        ),
    )(*operands)


def finish_kernel(sums_ref, up_ref, down_ref, *refs):
    *across, out_ref = refs
    total = sums_ref[0] + (up_ref[0].astype(F32) + down_ref[0].astype(F32))
    if across:
        total = total + across[0][...].astype(F32)
    out_ref[...] = total.astype(BF16)


def finished(*operands):
    return pl.pallas_call(
        finish_kernel,
        out_shape=jax.ShapeDtypeStruct((ROWS, ROWS), BF16),
        in_specs=[in_vmem()] * len(operands),
        out_specs=in_vmem(),
        compiler_params=params(),
        cost_estimate=pl.CostEstimate(
            flops=2 * ROWS * ROWS, bytes_accessed=8 * ROWS * ROWS, transcendentals=0
        ),
    )(*operands)


def shards(
    queries,
    cache_keys,
    cache_values,
    scale_index,
    scale_table,
    hist_lengths,
    span_offsets,
    new_keys,
    new_values,
    head_groups,
    out_weight,
):
    ctx, place = lax.axis_index("ctx"), lax.axis_index("head")
    y, xh = ctx // 2, ctx % 2
    z, xl, core = place // 4, (place // 2) % 2, place % 2

    length = hist_lengths[0]
    facts = head_groups.astype(BF16)
    facts = jnp.pad(facts[None], ((0, FACT_ROWS - 1), (0, DH - facts.shape[0])))
    q0 = jnp.transpose(queries, (1, 0, 2)).reshape(HEADS * ROWS, DH)
    q0 = jnp.concatenate([q0, facts])
    p0 = send(q0, dxh=1, dxl=1)
    q_down = send(q0, dy=1)
    q_up = send(q0, dy=-1)
    p_down = send(p0, dy=1)
    p_up = send(p0, dy=-1)
    q_far = send(q_up, dy=-1)
    sent_weight = send(out_weight, dcore=1)
    keys, values = loaded(cache_keys, cache_values)
    fresh, fresh_lse = fresh_part(
        head_groups,
        q0,
        jnp.transpose(new_keys, (1, 0, 2)),
        jnp.transpose(new_values, (1, 0, 2)),
    )
    pair_groups = p0[HEADS * ROWS, :HEADS].astype(I32)
    lengths = lax.all_to_all(
        jnp.broadcast_to(hist_lengths, (8,)), "ctx", split_axis=0, concat_axis=0, tiled=True
    )
    start = jnp.sum(jnp.where(jnp.arange(8) < ctx, lengths, 0))

    def counts(source_y, source_xh):
        source = (source_y % 4) * 2 + source_xh
        offsets = lax.dynamic_slice_in_dim(span_offsets, source * 2, 2)
        return jnp.clip(jnp.minimum(length, offsets - start), 0, SLOTS)

    def attend(groups, sources, source_xh, queries, previous=None, after=()):
        return history(
            groups,
            jnp.concatenate([counts(y + step, source_xh) for step in sources]),
            scale_index,
            scale_table,
            queries,
            keys,
            values,
            previous,
            after,
        )

    first = attend(pair_groups, (0,), 1 - xh, [p0])
    back = {0: (send(first, dxh=1, dxl=1), 0)}
    p_down, _ = lax.optimization_barrier((p_down, first))
    p_far = send(p_down, dy=1)
    for step, query in ((-1, p_down), (1, p_up), (2, p_far)):
        last = attend(pair_groups, (step,), 1 - xh, [query])
        back[step] = (send(last, dxh=1, dxl=1), 0)
    parts = []
    after = (last,)
    for step, query in ((0, q0), (-1, q_down), (1, q_up), (2, q_far)):
        part = attend(head_groups, (step,), xh, [query], back[step], after)
        after = (part,)
        parts.append(send(part, dy=step) if step else part)

    mine = combined(parts, fresh, fresh_lse)
    theirs = send(mine, dcore=1)

    def columns(steps):
        blocks = [(((z + step) % 8) * 2 + xl) ^ other for step, other in steps]
        return 2 * jnp.stack(blocks) + core

    def project(steps, kind, after):
        at = columns(steps)
        return projected(at, after, mine, theirs, out_weight, sent_weight, kind)

    at = columns([(4, 0), (4, 1)])
    first, fetched = projected_mine(at, mine, out_weight, sent_weight)
    first = projected_theirs(first, fetched, theirs)
    up = send(first[0:1], dz=1)
    down = send(first[1:2], dz=-1)
    steps = ((3, 0), (3, 1), (-3, 0), (-3, 1))
    sums = project(steps, F32, first)
    theirs_up, theirs_down = advanced(1, 3, sums, None, down)
    mine_up, mine_down = advanced(0, 2, sums, up, None)
    for step in (2, 1, 0):
        steps = ((step, 0), (step, 1), (-step, 0), (-step, 1))
        if step:
            sums = project(steps, F32, theirs_up)
        else:
            last_theirs = project([(0, 1)], F32, theirs_up)
            last_mine = project([(0, 0)], F32, last_theirs)
        theirs_up, theirs_down = send(theirs_up, dz=1), send(theirs_down, dz=-1)
        mine_up, mine_down = send(mine_up, dz=1), send(mine_down, dz=-1)
        if step:
            theirs_up, theirs_down = advanced(1, 3, sums, theirs_up, theirs_down)
            mine_up, mine_down = advanced(0, 2, sums, mine_up, mine_down)
    across = send(finished(last_theirs, theirs_up, theirs_down), dxl=1)
    return finished(last_mine, mine_up, mine_down, across)


def solution(mesh):
    placed = (
        P("ctx", "head", None),
        P(None, "ctx", None),
        P(None, "ctx", None),
        P(None, "ctx"),
        P(),
        P("ctx"),
        P(),
        P("ctx", None, None),
        P("ctx", None, None),
        P("head"),
        P("head", None),
    )
    return jax.shard_map(
        shards, mesh=mesh, in_specs=placed, out_specs=P("ctx", "head"), check_vma=False
    )
```
